512 devices in a mesh: expert: 128 (over z, y, core), tensor: 4 (over x).
Axes of the slice: x: 4, y: 8, z: 8, core: 2. Of those that a mesh axis runs over, the one named last changes fastest.
Arguments:
- cotangent: bfloat16 [16384, 2560], P('expert', 'tensor'), may hold values from -6 to 6
- route_first: int32 [16384, 6], P('expert'), may hold values from 0 to 127, all different within a row; in each aligned block of 128 rows (0 to 127, 128 to 255, ...) at most 9 rows name the same one
- gates_first: float32 [16384, 6], P('expert'), may hold values from 0.05 to 0.4
- hidden_first: bfloat16 [128, 1152, 768], P('expert', None, 'tensor'), may hold values from -6 to 6
- route_second: int32 [16384, 6], P('expert'), may hold values from 0 to 127, all different within a row; in each aligned block of 128 rows (0 to 127, 128 to 255, ...) at most 9 rows name the same one
- gates_second: float32 [16384, 6], P('expert'), may hold values from 0.05 to 0.4
- hidden_second: bfloat16 [128, 1152, 768], P('expert', None, 'tensor'), may hold values from -6 to 6
- master: float32 [128, 768, 2560], P('expert', None, 'tensor'), may hold values from -0.21875 to 0.21875
- moment_one: bfloat16 [128, 768, 2560], P('expert', None, 'tensor'), may hold values from -6 to 6
- moment_two: bfloat16 [128, 768, 2560], P('expert', None, 'tensor'), may hold values from 0.5 to 8
- old_plan: int32 [128], replicated, may hold values from 0 to 127, as said below
- new_plan: int32 [128], replicated, may hold values from 0 to 127, as said below
Outputs:
- layer_output: bfloat16 [16384, 2560], P('expert', 'tensor')
The draws below stay inside these ranges and needn't reach their ends.
Inputs may be any that keep to these rules, and one draw needn't show every extreme that they name: `route_first`: in the rows of one device no expert is named by more than 9 rows. `route_second`: in the rows of one device no expert is named by more than 9 rows. `old_plan`: a permutation: every expert stands in exactly one slot. `new_plan`: a permutation equal to old_plan except in 8 slots, whose experts trade places along one cycle.
All inputs are finite; a program needn't handle non-finite values.
Results may differ from the reference program's by a relative error of at most 0.0011.
The reference program's roundings to bfloat16 on the way count: a program that leaves them out, or rounds other values in their place, can miss the bound.
Values may be sent and summed in bfloat16 or wider, within the bound.
No kernel may reach another device: no remote copies, remote signals or barrier semaphores. Data moves between devices by JAX's collectives and lax.ppermute only.
A program may use at most 64 MiB of HBM per device.

```python
import math
import jax
import jax.numpy as jnp
import numpy as np
from jax import lax

D = 2560
HID = 768
TOP = 6
MOVES = 8
TOK_DEV = 128
EXPERTS = 128
TOKENS = 16384
CAP = 9
BUFROWS = 1152
N_EXPERT = 128


def plan_pair(key):
    first_key = jax.random.fold_in(key, 101)
    second_key = jax.random.fold_in(key, 102)
    before = jax.random.permutation(first_key, EXPERTS).astype(jnp.int32)
    chosen = jax.random.permutation(second_key, EXPERTS)[:MOVES].astype(jnp.int32)
    rotated = jnp.roll(chosen, 1)
    after = before.at[chosen].set(before[rotated])
    return (before, after)


def draw_old_plan(key, part):
    shared = plan_pair(key)
    return shared[0]


def draw_new_plan(key, part):
    shared = plan_pair(key)
    return shared[1]


def block_scale(rng, extent, split, low, high):
    def one(position, shards_of):
        steps = jax.random.uniform(jax.random.fold_in(jax.random.fold_in(rng, 6), position), (shards_of,), jnp.float32, low / len(split), high / len(split))
        return jnp.repeat(jnp.exp(steps), extent[position] // shards_of).reshape((-1,) + (1,) * (len(extent) - position - 1))

    loudness = one(*split[0])
    for cut in split[1:]:
        loudness = loudness * one(*cut)
    return loudness


def deal_out(own_key, own, number, rows, amount, top, bound, slope):
    order = jax.random.permutation(own_key, amount)
    packed, ordinary = portions_of(amount, rows * top, bound, slope, True), portions_of(amount, rows * top, bound, slope, False)
    places = jnp.arange(amount)

    def named(lengths, turn):
        used = int((lengths > 0).sum())
        fixed = max(1, used // 4)
        moved = fixed + (places - fixed + turn * (used - fixed)) % max(1, amount - fixed)
        return jnp.zeros((amount,), jnp.int32).at[order[jnp.where(places < fixed, places, moved)]].set(jnp.asarray(lengths, jnp.int32))

    lengths = jnp.where(number % 4 == 0, named(packed, number // 4), named(ordinary, number - number // 4 - 1))
    mixed = jax.random.permutation(jax.random.fold_in(own, 3), amount)
    giver, sink = mixed[0:amount // 2 * 2:2], mixed[1:amount // 2 * 2:2]
    slack = jnp.minimum(lengths[giver] - 1, bound - lengths[sink]) // 2
    slack = jnp.where((giver == order[0]) | (sink == order[0]) | (lengths[sink] == 0), 0, jnp.maximum(slack, 0))
    moved = jax.random.randint(jax.random.fold_in(own, 4), (amount // 2,), 0, 1 << 20) % (slack + 1)
    lengths = lengths.at[giver].add(-moved).at[sink].add(moved)
    members = jnp.searchsorted(jnp.cumsum(lengths), jnp.arange(rows * top), side="right").astype(jnp.int32)
    listing = members.reshape(top, rows).T
    listing = listing[jax.random.permutation(jax.random.fold_in(own, 1), rows)]
    turn = jax.random.randint(jax.random.fold_in(own, 2), (rows, 1), 0, top)
    return jnp.take_along_axis(listing, (jnp.arange(top)[None, :] + turn) % top, axis=1)


def portions_of(number_of, total, most, slope, full):
    weights = [(1 << 20) // math.isqrt(standing ** slope) + 1 for standing in range(1, number_of + 1)]
    largest = most if full else min(most, max(-(-total // number_of), total * weights[0] // sum(weights)))
    least = 1 if total - largest >= number_of - 1 else 0
    given, rest = [largest] + [least] * (number_of - 1), total - largest - least * (number_of - 1)
    while rest > 0:
        candidates = [i for i in range(1, number_of) if given[i] < largest] or [i for i in range(1, number_of) if given[i] < most]
        pool, remaining = sum([weights[i] for i in candidates]), rest
        for i in candidates:
            extra = min(most - given[i], max(1, remaining * weights[i] // pool), rest)
            given[i] = given[i] + extra
            rest = rest - extra
    return np.array(given)


def scatter_about(own_key, extent, width, reach, pieces=(), kind=jnp.bfloat16):
    drawn = jax.random.normal(own_key, extent, jnp.float32) * width
    if len(pieces) > 0:
        drawn = block_scale(own_key, extent, pieces, -0.22, 0.18) * drawn
    return jnp.clip(drawn, min=-reach, max=reach).astype(kind)


def setup_inputs(seed: int = 0) -> dict:
    seeds = jax.random.split(jax.random.key(seed), 13)
    cotangent = scatter_about(seeds[0], (TOKENS, D), 1.0, 6.0, ((0, 128), (1, 4)))
    route_first_keys = jax.random.split(jax.random.fold_in(seeds[1], 1), TOKENS // TOK_DEV)
    route_first_turns = jax.random.permutation(jax.random.fold_in(seeds[1], 3), TOKENS // TOK_DEV)
    route_first = jax.vmap(lambda own, number: deal_out(jax.random.fold_in(seeds[1], 2), own, number, TOK_DEV, EXPERTS, TOP, CAP, 2))(route_first_keys, route_first_turns).reshape((TOKENS, TOP))
    gates_first = jnp.clip(0.05 + 0.35 * jax.random.uniform(seeds[2], (TOKENS, TOP), jnp.float32) ** block_scale(seeds[2], (TOKENS, TOP), ((0, 128),), -0.2, 0.2), 0.05, 0.4)
    hidden_first = scatter_about(seeds[3], (EXPERTS, BUFROWS, HID), 1.0, 6.0, ((0, 128), (2, 4)))
    route_second_keys = jax.random.split(jax.random.fold_in(seeds[4], 1), TOKENS // TOK_DEV)
    route_second_turns = jax.random.permutation(jax.random.fold_in(seeds[4], 3), TOKENS // TOK_DEV)
    route_second = jax.vmap(lambda own, number: deal_out(jax.random.fold_in(seeds[4], 2), own, number, TOK_DEV, EXPERTS, TOP, CAP, 2))(route_second_keys, route_second_turns).reshape((TOKENS, TOP))
    gates_second = jnp.clip(0.05 + 0.35 * jax.random.uniform(seeds[5], (TOKENS, TOP), jnp.float32) ** block_scale(seeds[5], (TOKENS, TOP), ((0, 128),), -0.2, 0.2), 0.05, 0.4)
    hidden_second = scatter_about(seeds[6], (EXPERTS, BUFROWS, HID), 1.0, 6.0, ((0, 128), (2, 4)))
    master = scatter_about(seeds[7], (EXPERTS, HID, D), HID ** -0.5, 0.21875, ((0, 128), (2, 4)), jnp.float32)
    moment_one = scatter_about(seeds[8], (EXPERTS, HID, D), 1.0, 6.0, ((0, 128), (2, 4)))
    moment_two = jnp.clip(jnp.exp(math.log(8.0) - 2.7725887 * jax.random.uniform(seeds[9], (EXPERTS, HID, D), jnp.float32) ** block_scale(seeds[9], (EXPERTS, HID, D), ((0, 128), (2, 4)), -0.2, 0.2)), 0.5, 8.0).astype(jnp.bfloat16)
    old_plan = draw_old_plan(jax.random.fold_in(seeds[12], 71), 0)
    new_plan = draw_new_plan(jax.random.fold_in(seeds[12], 71), 0)
    return dict(cotangent=cotangent, route_first=route_first, gates_first=gates_first, hidden_first=hidden_first, route_second=route_second, gates_second=gates_second, hidden_second=hidden_second, master=master, moment_one=moment_one, moment_two=moment_two, old_plan=old_plan, new_plan=new_plan)


BETA_ONE = 0.9
BETA_TWO = 0.95
CORRECT_ONE = 1.0 - 0.9 ** 10
CORRECT_TWO = 1.0 - 0.95 ** 10
LEARN_RATE = 0.04
WEIGHT_DECAY = 0.1
EPSILON = 1e-08

def slot_ranking(routing):
    blocks = routing.reshape(N_EXPERT, TOK_DEV * TOP)
    labels = jnp.arange(EXPERTS, dtype=jnp.int32)

    def within(block_ids):
        onehot = (block_ids[:, None] == labels[None, :]).astype(jnp.int32)
        before = jnp.cumsum(onehot, axis=0) - onehot
        return lax.optimization_barrier(jnp.sum(before * onehot, axis=1)).astype(jnp.int32)
    return lax.map(within, blocks).reshape(TOKENS * TOP)

def inverse(placement_plan):
    labels = jnp.arange(EXPERTS, dtype=jnp.int32)
    return jnp.zeros((EXPERTS,), jnp.int32).at[placement_plan].set(labels)

def buffer_rows(routing, placement_plan):
    slot_ids = inverse(placement_plan)[routing.reshape(TOKENS * TOP)]
    sources = (jnp.arange(TOKENS * TOP, dtype=jnp.int32) // (TOK_DEV * TOP)).astype(jnp.int32)
    return (slot_ids * BUFROWS + sources * CAP + slot_ranking(routing)).astype(jnp.int32)

def adam_weight(master, moment_one, moment_two, gradient):
    moment_new = BETA_ONE * moment_one.astype(jnp.float32) + (1.0 - BETA_ONE) * gradient
    second = BETA_TWO * moment_two.astype(jnp.float32) + (1.0 - BETA_TWO) * gradient * gradient
    ratio = moment_new / CORRECT_ONE / (jnp.sqrt(second / CORRECT_TWO) + EPSILON)
    updated = master - LEARN_RATE * (ratio + WEIGHT_DECAY * master)
    return updated.astype(jnp.bfloat16)

def reference(cotangent, route_first, gates_first, hidden_first, route_second, gates_second, hidden_second, master, moment_one, moment_two, old_plan, new_plan):
    target = buffer_rows(route_first, old_plan)
    scaled = (gates_first[:, :, None] * cotangent[:, None, :].astype(jnp.float32)).astype(jnp.bfloat16)
    scaled = scaled.reshape(TOKENS * TOP, D)
    received = jnp.zeros((EXPERTS * BUFROWS, D), jnp.bfloat16).at[target].set(scaled)
    received = received.reshape(EXPERTS, BUFROWS, D)

    def update(slot_id):
        gradient = jnp.dot(hidden_first[slot_id].T, received[slot_id], preferred_element_type=jnp.float32)
        return adam_weight(master[slot_id], moment_one[slot_id], moment_two[slot_id], gradient)
    weights = lax.map(update, jnp.arange(EXPERTS, dtype=jnp.int32))
    source_slot = inverse(old_plan)[new_plan]

    def forward(slot_id):
        return jnp.dot(hidden_second[slot_id], weights[source_slot[slot_id]], preferred_element_type=jnp.float32).astype(jnp.bfloat16)
    produced = lax.map(forward, jnp.arange(EXPERTS, dtype=jnp.int32)).reshape(EXPERTS * BUFROWS, D)
    picked = produced[buffer_rows(route_second, new_plan)].reshape(TOKENS, TOP, D)
    summed = jnp.zeros((TOKENS, D), jnp.float32)
    for column in range(TOP):
        summed = summed + gates_second[:, column, None] * picked[:, column, :].astype(jnp.float32)
    return summed.astype(jnp.bfloat16)
```

```python
import jax
import jax.numpy as jnp
from jax import lax
from jax.experimental import pallas as pl
from jax.experimental.pallas import tpu as pltpu
from jax.sharding import PartitionSpec as P

BETA_ONE = 0.9
BETA_TWO = 0.95
CORRECT_ONE = 1.0 - 0.9**10
CORRECT_TWO = 1.0 - 0.95**10
LEARN_RATE = 0.04
WEIGHT_DECAY = 0.1
EPSILON = 1e-08

EXP = 128
TOK = 128
TOP = 6
CAP = 9
ROWS = EXP * CAP
MAIN = EXP * 8
HID = 768
HPART = 192
COLS = 640
WIDE = 768
PIECES = 108
PROWS = PIECES * 16
NONE = 99.0
VMEM_LIMIT = 48 * 1024 * 1024
F32 = jnp.float32
BF16 = jnp.bfloat16

NN = (((1,), (0,)), ((), ()))
NT = (((1,), (1,)), ((), ()))


def params():
    return pltpu.CompilerParams(vmem_limit_bytes=VMEM_LIMIT)


def iota(shape, dim):
    return lax.broadcasted_iota(jnp.int32, shape, dim)


def mm(a, b, dims=NN):
    return lax.dot_general(a, b, dims, preferred_element_type=F32)


def thirds(x):
    high = x.astype(BF16)
    rest = x - high.astype(F32)
    mid = rest.astype(BF16)
    low = (rest - mid.astype(F32)).astype(BF16)
    return high, mid, low


def routed(route, gates, plan):
    diag = iota((EXP, EXP), 0) == iota((EXP, EXP), 1)
    column = jnp.sum(jnp.where(diag, plan.astype(F32), 0.0), axis=1, keepdims=True)
    named = route.astype(F32)
    member = jnp.zeros((EXP, TOK), F32)
    gate = jnp.zeros((EXP, TOK), F32)
    for k in range(TOP):
        same = named[k : k + 1, :] == column
        member = jnp.where(same, 1.0, member)
        gate = jnp.where(same, gates[k : k + 1, :], gate)
    earlier = (iota((TOK, TOK), 0) < iota((TOK, TOK), 1)).astype(F32).astype(BF16)
    rank = mm(member.astype(BF16), earlier)
    return jnp.where(member > 0.0, rank, NONE), gate


def onehot(mask):
    return jnp.where(mask, 1.0, 0.0).astype(BF16)


def main_pick(block):
    r = iota((128, 256), 0)
    return onehot(iota((128, 256), 1) == 16 * block + (r // 8) * 9 + r % 8)


def last_pick():
    return onehot(iota((EXP, ROWS), 1) == iota((EXP, ROWS), 0) * 9 + 8)


def prepare_second(h_ref, out_ref):
    first = h_ref[0:128, :]
    second = h_ref[128:192, :]
    blank = jnp.zeros_like(second)
    low = jnp.concatenate([second, blank], axis=0)
    high = jnp.concatenate([blank, second], axis=0)
    pick = [main_pick(b) for b in range(8)]
    last = last_pick()
    for b in range(8):
        win = slice(128 * b, 128 * b + 256)
        out_ref[128 * b : 128 * b + 128, :] = mm(pick[b], first[:, win], NT).astype(BF16)
    out_ref[MAIN:ROWS, :] = mm(last, first, NT).astype(BF16)
    for b in range(4):
        win_low = slice(128 * b, 128 * b + 256)
        win_high = slice(128 * b + 512, 128 * b + 768)
        both = mm(pick[b], low[:, win_low], NT) + mm(pick[b + 4], high[:, win_high], NT)
        out_ref[ROWS + 128 * b : ROWS + 128 * b + 128, :] = both.astype(BF16)
    both = mm(last[0:64], low, NT) + mm(last[64:128], high, NT)
    out_ref[ROWS + 512 : PROWS, :] = both.astype(BF16)
    out_ref[PROWS:, :] = jnp.zeros((128 * 16 - PROWS, 128), BF16)


def prepare_first(h_ref, out_ref):
    for b in range(8):
        win = slice(128 * b, 128 * b + 256)
        out_ref[:, 128 * b : 128 * b + 128] = mm(h_ref[:, win], main_pick(b), NT).astype(BF16)
    out_ref[:, MAIN:ROWS] = mm(h_ref[...], last_pick(), NT).astype(BF16)


def build_rows(route_ref, gates_ref, plan_ref, tokens_ref, out_ref, extra):
    rank, gate = routed(route_ref[...], gates_ref[...], plan_ref[...])
    tokens = tokens_ref[...]
    high, mid, low = thirds(gate)
    code = rank.astype(BF16)
    for b in range(4):
        r = iota((256, EXP), 0)
        spread = onehot(iota((256, EXP), 1) == 32 * b + r // 8)
        here = mm(spread, code) == (r % 8).astype(F32)
        gates_here = (mm(spread, high) + mm(spread, mid)) + mm(spread, low)
        scale = jnp.sum(jnp.where(here, gates_here, 0.0), axis=1, keepdims=True)
        rows = mm(onehot(here), tokens)
        out_ref[256 * b : 256 * b + 256, 0:COLS] = (scale * rows).astype(BF16)
    here = rank == 8.0
    scale = jnp.sum(jnp.where(here, gate, 0.0), axis=1, keepdims=True)
    rows = (scale * mm(onehot(here), tokens)).astype(BF16).astype(F32)
    extra[...] = jnp.zeros_like(extra)
    for q in range(5):
        extra[pl.ds(q, EXP, stride=8), :] = rows[:, 128 * q : 128 * q + 128]
    out_ref[:, COLS:WIDE] = extra[...].astype(BF16)


def choose(source_ref, in_ref, out_ref):
    def body(slot, carry):
        out_ref[slot] = in_ref[source_ref[slot]]
        return carry

    lax.fori_loop(0, EXP, body, 0, unroll=8)


def last_rows(payload_ref, extra):
    extra[...] = payload_ref[:, COLS:WIDE].astype(F32)
    return jnp.concatenate(
        [extra[pl.ds(q, EXP, stride=8), :] for q in range(5)], axis=1
    ).astype(BF16)


def update(hidden_ref, payload_ref, master_ref, one_ref, two_ref, out_ref, extra, last):
    @pl.when(pl.program_id(0) == 0)
    def _():
        last[...] = last_rows(payload_ref, extra)

    gradient = mm(hidden_ref[:, 0:MAIN], payload_ref[:, 0:COLS]) + mm(
        hidden_ref[:, MAIN:ROWS], last[...]
    )
    master = master_ref[...]
    moment_new = BETA_ONE * one_ref[...].astype(F32) + (1.0 - BETA_ONE) * gradient
    second = BETA_TWO * two_ref[...].astype(F32) + (1.0 - BETA_TWO) * gradient * gradient
    ratio = moment_new / CORRECT_ONE / (jnp.sqrt(second / CORRECT_TWO) + EPSILON)
    updated = master - LEARN_RATE * (ratio + WEIGHT_DECAY * master)
    out_ref[...] = updated.astype(BF16)


def forward(hidden_ref, weight_ref, out_ref, extra):
    def part(t, low, high):
        return weight_ref[t * HPART + low : t * HPART + high, :]

    blank = jnp.zeros((64, COLS), BF16)
    pairs = [jnp.concatenate([part(t, 0, 128), part(t + 1, 0, 128)], axis=0) for t in (0, 2)]
    lows = [
        jnp.concatenate([part(t, 128, 192), blank, part(t + 1, 128, 192), blank], axis=0)
        for t in (0, 2)
    ]
    highs = [
        jnp.concatenate([blank, part(t, 128, 192), blank, part(t + 1, 128, 192)], axis=0)
        for t in (0, 2)
    ]

    def rows(at, count, packed_at, weights):
        total = None
        for n, t in enumerate((0, 2)):
            one = jnp.concatenate(
                [hidden_ref[t, at : at + count, :], hidden_ref[t + 1, at : at + count, :]], axis=1
            )
            two = jnp.concatenate(
                [
                    hidden_ref[t, packed_at : packed_at + count, :],
                    hidden_ref[t + 1, packed_at : packed_at + count, :],
                ],
                axis=1,
            )
            term = mm(one, pairs[n]) + mm(two, weights[n])
            total = term if total is None else total + term
        return total.astype(BF16)

    for b in range(4):
        for half, weights in ((0, lows), (512, highs)):
            at = half + 128 * b
            out_ref[at : at + 128, 0:COLS] = rows(at, 128, ROWS + 128 * b, weights)
    last = jnp.concatenate(
        [
            rows(MAIN, 64, ROWS + 512, lows),
            rows(MAIN + 64, 64, ROWS + 512, highs),
        ],
        axis=0,
    ).astype(F32)
    extra[...] = jnp.zeros_like(extra)
    for q in range(5):
        extra[pl.ds(q, EXP, stride=8), :] = last[:, 128 * q : 128 * q + 128]
    out_ref[:, COLS:WIDE] = extra[...].astype(BF16)


def mixing(route_ref, gates_ref, plan_ref, main_ref, last_ref):
    rank, gate = routed(route_ref[...], gates_ref[...], plan_ref[...])
    rank = rank.T
    gate = gate.T
    code = rank.astype(BF16)
    parts = thirds(gate)
    for b in range(4):
        c = iota((EXP, 256), 1)
        spread = onehot(iota((EXP, 256), 0) == 32 * b + c // 8)
        here = mm(code, spread) == (c % 8).astype(F32)
        for n, part in enumerate(parts):
            main_ref[128 * n : 128 * n + 128, 256 * b : 256 * b + 256] = jnp.where(
                here, mm(part, spread), 0.0
            ).astype(BF16)
    for n, part in enumerate(parts):
        last_ref[128 * n : 128 * n + 128, :] = jnp.where(
            rank == 8.0, part.astype(F32), 0.0
        ).astype(BF16)


def combine(main_ref, last_ref, payload_ref, out_ref, extra):
    total = mm(main_ref[...], payload_ref[:, 0:COLS]) + mm(
        last_ref[...], last_rows(payload_ref, extra)
    )
    out_ref[...] = (total[0:128] + (total[128:256] + total[256:384])).astype(BF16)


def shape(*extents, dtype=BF16):
    return jax.ShapeDtypeStruct(extents, dtype)


def exchange(x):
    return lax.all_to_all(x, "expert", split_axis=0, concat_axis=0, tiled=True)


def shards(
    cotangent,
    route_first,
    gates_first,
    hidden_first,
    route_second,
    gates_second,
    hidden_second,
    master,
    moment_one,
    moment_two,
    old_plan,
    new_plan,
):
    labels = jnp.arange(EXP, dtype=jnp.int32)
    plan = old_plan.reshape(1, EXP)
    source = jnp.sum(
        jnp.where(new_plan[None, :] == old_plan[:, None], labels[None, :], 0), axis=1
    )
    extra = pltpu.VMEM((MAIN, 128), F32)

    with jax.named_scope("second_hidden_out"):
        pieces = pl.pallas_call(
            prepare_second, out_shape=shape(EXP * 16, 128), compiler_params=params()
        )(hidden_second[0].T)
        spread = exchange(pieces.reshape(EXP, 16, 128))

    with jax.named_scope("dispatch"):
        rows = pl.pallas_call(
            build_rows,
            out_shape=shape(MAIN, WIDE),
            scratch_shapes=[extra],
            compiler_params=params(),
        )(route_first.T, gates_first.T, plan, cotangent)
        arrived = exchange(rows.reshape(EXP, 8, WIDE)).reshape(MAIN, WIDE)

    with jax.named_scope("first_hidden"):
        first = pl.pallas_call(
            prepare_first, out_shape=shape(HPART, ROWS), compiler_params=params()
        )(hidden_first[0].T)
        first = lax.all_gather(first, "tensor", axis=0, tiled=True)

    with jax.named_scope("second_hidden_in"):
        chosen = pl.pallas_call(
            choose,
            out_shape=shape(EXP, 16, 128),
            in_specs=[
                pl.BlockSpec(memory_space=pltpu.SMEM),
                pl.BlockSpec(memory_space=pltpu.VMEM),
            ],
            compiler_params=params(),
        )(source, spread)
        mine = exchange(chosen)[:PIECES].reshape(PROWS, 128)
        second = lax.all_gather(mine, "tensor", axis=0)

    with jax.named_scope("mixing"):
        mix, mix_last = pl.pallas_call(
            mixing,
            out_shape=(shape(3 * TOK, MAIN), shape(3 * TOK, EXP)),
            compiler_params=params(),
        )(route_second.T, gates_second.T, plan)

    with jax.named_scope("update"):
        step = 128
        weight = pl.pallas_call(
            update,
            grid=(HID // step,),
            in_specs=[
                pl.BlockSpec((step, ROWS), lambda i: (i, 0)),
                pl.BlockSpec((MAIN, WIDE), lambda i: (0, 0)),
                pl.BlockSpec((step, COLS), lambda i: (i, 0)),
                pl.BlockSpec((step, COLS), lambda i: (i, 0)),
                pl.BlockSpec((step, COLS), lambda i: (i, 0)),
            ],
            out_specs=pl.BlockSpec((step, COLS), lambda i: (i, 0)),
            out_shape=shape(HID, COLS),
            scratch_shapes=[extra, pltpu.VMEM((EXP, COLS), BF16)],
            compiler_params=params(),
        )(first, arrived, master[0], moment_one[0], moment_two[0])

    with jax.named_scope("forward"):
        produced = pl.pallas_call(
            forward,
            out_shape=shape(MAIN, WIDE),
            scratch_shapes=[extra],
            compiler_params=params(),
        )(second, weight)
        returned = exchange(produced.reshape(EXP, 8, WIDE)).reshape(MAIN, WIDE)

    with jax.named_scope("combine"):
        return pl.pallas_call(
            combine,
            out_shape=shape(TOK, COLS),
            scratch_shapes=[extra],
            compiler_params=params(),
        )(mix, mix_last, returned)


def solution(mesh):
    placed = (
        P("expert", "tensor"),
        P("expert", None),
        P("expert", None),
        P("expert", None, "tensor"),
        P("expert", None),
        P("expert", None),
        P("expert", None, "tensor"),
        P("expert", None, "tensor"),
        P("expert", None, "tensor"),
        P("expert", None, "tensor"),
        P(),
        P(),
    )
    return jax.shard_map(
        shards, mesh=mesh, in_specs=placed, out_specs=P("expert", "tensor"), check_vma=False
    )
```

```python
import jax
import jax.numpy as jnp
from jax import lax
from jax.experimental import pallas as pl
from jax.experimental.pallas import tpu as pltpu
from jax.sharding import PartitionSpec as P

BETA_ONE = 0.9
BETA_TWO = 0.95
CORRECT_ONE = 1.0 - 0.9**10
CORRECT_TWO = 1.0 - 0.95**10
LEARN_RATE = 0.04
WEIGHT_DECAY = 0.1
EPSILON = 1e-08
KEEP = 1.0 - LEARN_RATE * WEIGHT_DECAY
ONE_OLD = LEARN_RATE * BETA_ONE / CORRECT_ONE
ONE_NEW = LEARN_RATE * (1.0 - BETA_ONE) / CORRECT_ONE
TWO_OLD = BETA_TWO / CORRECT_TWO
TWO_NEW = (1.0 - BETA_TWO) / CORRECT_TWO

EXP = 128
TOK = 128
TOP = 6
CAP = 9
ROWS = EXP * CAP
MAIN = EXP * 8
HID = 768
HPART = 192
COLS = 640
WIDE = 768
PROWS = ROWS * HPART // 128
NONE = 99.0
LEG = (7, 2, 128)
MOVES = 8
STEP = 256
HALF = ROWS // 2
F32 = jnp.float32
BF16 = jnp.bfloat16

NN = (((1,), (0,)), ((), ()))
NT = (((1,), (1,)), ((), ()))


def params(limit=16):
    return pltpu.CompilerParams(vmem_limit_bytes=limit * 1024 * 1024)


def iota(shape, dim):
    return lax.broadcasted_iota(jnp.int32, shape, dim)


def mm(a, b, dims=NN):
    return lax.dot_general(a, b, dims, preferred_element_type=F32)


def thirds(x):
    high = x.astype(BF16)
    rest = x - high.astype(F32)
    mid = rest.astype(BF16)
    low = (rest - mid.astype(F32)).astype(BF16)
    return high, mid, low


def routed(route, gates, plan):
    diag = iota((EXP, EXP), 0) == iota((EXP, EXP), 1)
    column = jnp.sum(jnp.where(diag, plan.astype(F32), 0.0), axis=1, keepdims=True)
    named = route.astype(F32)
    member = jnp.zeros((EXP, TOK), F32)
    gate = jnp.zeros((EXP, TOK), F32)
    for k in range(TOP):
        same = named[k : k + 1, :] == column
        member = jnp.where(same, 1.0, member)
        gate = jnp.where(same, gates[k : k + 1, :], gate)
    earlier = (iota((TOK, TOK), 0) < iota((TOK, TOK), 1)).astype(F32).astype(BF16)
    rank = mm(member.astype(BF16), earlier)
    return jnp.where(member > 0.0, rank, NONE), gate


def onehot(mask):
    return jnp.where(mask, 1.0, 0.0).astype(BF16)


def main_pick(block):
    r = iota((128, 256), 0)
    return onehot(iota((128, 256), 1) == 16 * block + (r // 8) * 9 + r % 8)


def last_pick():
    return onehot(iota((EXP, ROWS), 1) == iota((EXP, ROWS), 0) * 9 + 8)


def prepare_second(h_ref, out_ref):
    first = h_ref[0:128, :]
    second = h_ref[128:192, :]
    blank = jnp.zeros_like(second)
    low = jnp.concatenate([second, blank], axis=0)
    high = jnp.concatenate([blank, second], axis=0)
    pick = [main_pick(b) for b in range(8)]
    last = last_pick()
    for b in range(8):
        win = slice(128 * b, 128 * b + 256)
        at = 128 * b + 64 * (b // 4)
        out_ref[at : at + 128, :] = mm(pick[b], first[:, win], NT).astype(BF16)
    ends = mm(last, first, NT).astype(BF16)
    out_ref[512:HALF, :] = ends[0:64]
    out_ref[HALF + 512 : ROWS, :] = ends[64:128]
    for b in range(4):
        win_low = slice(128 * b, 128 * b + 256)
        win_high = slice(128 * b + 512, 128 * b + 768)
        both = mm(pick[b], low[:, win_low], NT) + mm(pick[b + 4], high[:, win_high], NT)
        out_ref[ROWS + 128 * b : ROWS + 128 * b + 128, :] = both.astype(BF16)
    both = mm(last[0:64], low, NT) + mm(last[64:128], high, NT)
    out_ref[ROWS + 512 : PROWS, :] = both.astype(BF16)


def prepare_first(h_ref, out_ref):
    for b in range(8):
        win = slice(128 * b, 128 * b + 256)
        out_ref[:, 128 * b : 128 * b + 128] = mm(h_ref[:, win], main_pick(b), NT).astype(BF16)
    out_ref[:, MAIN:ROWS] = mm(h_ref[...], last_pick(), NT).astype(BF16)


def build_rows(route_ref, gates_ref, plan_ref, tokens_ref, out_ref, extra):
    rank, gate = routed(route_ref[...], gates_ref[...], plan_ref[...])
    tokens = tokens_ref[...]
    high, mid, low = thirds(gate)
    code = rank.astype(BF16)
    for b in range(4):
        r = iota((256, EXP), 0)
        spread = onehot(iota((256, EXP), 1) == 32 * b + r // 8)
        here = mm(spread, code) == (r % 8).astype(F32)
        gates_here = (mm(spread, high) + mm(spread, mid)) + mm(spread, low)
        scale = jnp.sum(jnp.where(here, gates_here, 0.0), axis=1, keepdims=True)
        rows = mm(onehot(here), tokens)
        out_ref[256 * b : 256 * b + 256, 0:COLS] = (scale * rows).astype(BF16)
    here = rank == 8.0
    scale = jnp.sum(jnp.where(here, gate, 0.0), axis=1, keepdims=True)
    rows = (scale * mm(onehot(here), tokens)).astype(BF16).astype(F32)
    extra[...] = jnp.zeros_like(extra)
    for q in range(5):
        extra[pl.ds(q, EXP, stride=8), :] = rows[:, 128 * q : 128 * q + 128]
    out_ref[:, COLS:WIDE] = extra[...].astype(BF16)


def choose(to_ref, from_ref, in_ref, out_ref):
    out_ref[...] = in_ref[...]
    for m in range(MOVES):
        out_ref[to_ref[m]] = in_ref[from_ref[m]]


def last_rows(payload_ref, extra):
    extra[...] = payload_ref[:, COLS:WIDE].astype(F32)
    return jnp.concatenate(
        [extra[pl.ds(q, EXP, stride=8), :] for q in range(5)], axis=1
    ).astype(BF16)


def finish(
    payload_ref, hidden_hbm, master_hbm, one_hbm, two_hbm, second_hbm, out_ref,
    hidden, master, one, two, second, weight, last, extra, sems,
):
    sources = (hidden_hbm, master_hbm, one_hbm, two_hbm)
    targets = (hidden, master, one, two)
    steps = HID // STEP
    copies = []
    for n in range(steps):
        at = pl.ds(n * STEP, STEP)
        copies.append(
            [
                pltpu.make_async_copy(sources[i].at[at], targets[i].at[at], sems.at[4 * n + i])
                for i in range(4)
            ]
        )
        for copy in copies[n]:
            copy.start()
    rest = pltpu.make_async_copy(second_hbm, second, sems.at[4 * steps])
    rest.start()

    last[...] = last_rows(payload_ref, extra)
    for n in range(steps):
        at = slice(n * STEP, n * STEP + STEP)
        for copy in copies[n]:
            copy.wait()
        gradient = mm(hidden[at, 0:MAIN], payload_ref[:, 0:COLS]) + mm(
            hidden[at, MAIN:ROWS], last[...]
        )
        moment_new = ONE_OLD * one[at].astype(F32) + ONE_NEW * gradient
        moment_two = TWO_OLD * two[at].astype(F32) + TWO_NEW * gradient * gradient
        updated = KEEP * master[at] - moment_new / (jnp.sqrt(moment_two) + EPSILON)
        weight[at, :] = updated.astype(BF16)
    rest.wait()

    def part(t, low, high, cols):
        return weight[t * HPART + low : t * HPART + high, cols]

    def pair(t, rows):
        return jnp.concatenate([second[t, rows, :], second[t + 1, rows, :]], axis=1)

    extra[...] = jnp.zeros_like(extra)
    packed = [pair(t, slice(ROWS, PROWS)) for t in (0, 2)]
    for half in range(2):
        rows = slice(HALF * half, HALF * half + HALF)
        whole = [pair(t, rows) for t in (0, 2)]
        for start, stop in ((0, 256), (256, 512), (512, 640)):
            cols = slice(start, stop)
            blank = jnp.zeros((64, stop - start), BF16)
            total = None
            for n, t in enumerate((0, 2)):
                both = jnp.concatenate([part(t, 0, 128, cols), part(t + 1, 0, 128, cols)], axis=0)
                ends = [part(t, 128, 192, cols), part(t + 1, 128, 192, cols)]
                if half == 0:
                    ends = [ends[0], blank, ends[1], blank]
                else:
                    ends = [blank, ends[0], blank, ends[1]]
                term = mm(whole[n], both) + mm(packed[n], jnp.concatenate(ends, axis=0))
                total = term if total is None else total + term
            total = total.astype(BF16)
            out_ref[512 * half : 512 * half + 512, cols] = total[0:512]
            ends = total[512:HALF].astype(F32)
            for q in range(start // 128, stop // 128):
                at = 128 * q - start
                extra[pl.ds(512 * half + q, 64, stride=8), :] = ends[:, at : at + 128]
    out_ref[:, COLS:WIDE] = extra[...].astype(BF16)


def mixing(route_ref, gates_ref, plan_ref, main_ref, last_ref):
    rank, gate = routed(route_ref[...], gates_ref[...], plan_ref[...])
    rank = rank.T
    gate = gate.T
    code = rank.astype(BF16)
    parts = thirds(gate)
    for b in range(4):
        c = iota((EXP, 256), 1)
        spread = onehot(iota((EXP, 256), 0) == 32 * b + c // 8)
        here = mm(code, spread) == (c % 8).astype(F32)
        for n, part in enumerate(parts):
            main_ref[128 * n : 128 * n + 128, 256 * b : 256 * b + 256] = jnp.where(
                here, mm(part, spread), 0.0
            ).astype(BF16)
    for n, part in enumerate(parts):
        last_ref[128 * n : 128 * n + 128, :] = jnp.where(
            rank == 8.0, part.astype(F32), 0.0
        ).astype(BF16)


def combine(main_ref, last_ref, payload_ref, out_ref, extra):
    total = mm(main_ref[...], payload_ref[:, 0:COLS]) + mm(
        last_ref[...], last_rows(payload_ref, extra)
    )
    out_ref[...] = (total[0:128] + (total[128:256] + total[256:384])).astype(BF16)


def shape(*extents, dtype=BF16):
    return jax.ShapeDtypeStruct(extents, dtype)


def exchange(x):
    return lax.all_to_all(x, "expert", split_axis=0, concat_axis=0, tiled=True)


def shards(
    cotangent,
    route_first,
    gates_first,
    hidden_first,
    route_second,
    gates_second,
    hidden_second,
    master,
    moment_one,
    moment_two,
    old_plan,
    new_plan,
):
    labels = jnp.arange(EXP, dtype=jnp.int32)
    plan = old_plan.reshape(1, EXP)
    moved = old_plan != new_plan
    order = jnp.sum(jnp.where((labels[None, :] < labels[:, None]) & moved[None, :], 1, 0), axis=1)
    chosen = (order[None, :] == labels[:MOVES, None]) & moved[None, :]
    to = jnp.sum(jnp.where(chosen, labels[None, :], 0), axis=1)
    source = jnp.sum(jnp.where(new_plan[None, :] == old_plan[:, None], labels[None, :], 0), axis=1)
    origin = jnp.sum(jnp.where(labels[None, :] == to[:, None], source[None, :], 0), axis=1)
    extra = pltpu.VMEM((MAIN, 128), F32)
    hbm = pl.BlockSpec(memory_space=pltpu.HBM)
    smem = pl.BlockSpec(memory_space=pltpu.SMEM)
    vmem = pl.BlockSpec(memory_space=pltpu.VMEM)

    with jax.named_scope("second_hidden_out"):
        tiles = hidden_second[0].T.reshape(24, 8, 9, 128).transpose(0, 2, 1, 3)
        tiles = jnp.pad(tiles.reshape(PROWS, 128), ((0, EXP * 14 - PROWS), (0, 0)))
        spread = exchange(tiles.reshape(EXP, *LEG))

    with jax.named_scope("dispatch"):
        rows = pl.pallas_call(
            build_rows,
            out_shape=shape(MAIN, WIDE),
            scratch_shapes=[extra],
            compiler_params=params(),
        )(route_first.T, gates_first.T, plan, cotangent)
        arrived = exchange(rows.reshape(EXP, 8, WIDE)).reshape(MAIN, WIDE)

    with jax.named_scope("first_hidden"):
        first = lax.all_gather(hidden_first[0].T, "tensor", axis=0, tiled=True)
        first = pl.pallas_call(
            prepare_first, out_shape=shape(HID, ROWS), compiler_params=params()
        )(first)

    with jax.named_scope("second_hidden_in"):
        kept = pl.pallas_call(
            choose,
            out_shape=shape(EXP, *LEG),
            in_specs=[smem, smem, vmem],
            compiler_params=params(),
        )(to, origin, spread)
        mine = exchange(kept).reshape(EXP * 14, 128)[:PROWS]
        mine = mine.reshape(24, 9, 8, 128).transpose(0, 2, 1, 3).reshape(HPART, ROWS)
        mine = pl.pallas_call(
            prepare_second, out_shape=shape(PROWS, 128), compiler_params=params()
        )(mine)
        second = lax.all_gather(mine, "tensor", axis=0)

    with jax.named_scope("mixing"):
        mix, mix_last = pl.pallas_call(
            mixing,
            out_shape=(shape(3 * TOK, MAIN), shape(3 * TOK, EXP)),
            compiler_params=params(),
        )(route_second.T, gates_second.T, plan)

    with jax.named_scope("finish"):
        produced = pl.pallas_call(
            finish,
            in_specs=[vmem, hbm, hbm, hbm, hbm, hbm],
            out_shape=shape(MAIN, WIDE),
            scratch_shapes=[
                pltpu.VMEM((HID, ROWS), BF16),
                pltpu.VMEM((HID, COLS), F32),
                pltpu.VMEM((HID, COLS), BF16),
                pltpu.VMEM((HID, COLS), BF16),
                pltpu.VMEM((4, PROWS, 128), BF16),
                pltpu.VMEM((HID, COLS), BF16),
                pltpu.VMEM((EXP, COLS), BF16),
                extra,
                pltpu.SemaphoreType.DMA((4 * (HID // STEP) + 1,)),
            ],
            compiler_params=params(48),
        )(arrived, first, master[0], moment_one[0], moment_two[0], second)
        returned = exchange(produced.reshape(EXP, 8, WIDE)).reshape(MAIN, WIDE)

    with jax.named_scope("combine"):
        return pl.pallas_call(
            combine,
            out_shape=shape(TOK, COLS),
            scratch_shapes=[extra],
            compiler_params=params(),
        )(mix, mix_last, returned)


def solution(mesh):
    placed = (
        P("expert", "tensor"),
        P("expert", None),
        P("expert", None),
        P("expert", None, "tensor"),
        P("expert", None),
        P("expert", None),
        P("expert", None, "tensor"),
        P("expert", None, "tensor"),
        P("expert", None, "tensor"),
        P("expert", None, "tensor"),
        P(),
        P(),
    )
    return jax.shard_map(
        shards, mesh=mesh, in_specs=placed, out_specs=P("expert", "tensor"), check_vma=False
    )
```

```python
import jax
import jax.numpy as jnp
from jax import lax
from jax.experimental import pallas as pl
from jax.experimental.pallas import tpu as pltpu
from jax.sharding import PartitionSpec as P

BETA_ONE = 0.9
BETA_TWO = 0.95
CORRECT_ONE = 1.0 - 0.9**10
CORRECT_TWO = 1.0 - 0.95**10
LEARN_RATE = 0.04
WEIGHT_DECAY = 0.1
EPSILON = 1e-08
KEEP = 1.0 - LEARN_RATE * WEIGHT_DECAY
ONE_OLD = LEARN_RATE * BETA_ONE / CORRECT_ONE
ONE_NEW = LEARN_RATE * (1.0 - BETA_ONE) / CORRECT_ONE
TWO_OLD = BETA_TWO / CORRECT_TWO
TWO_NEW = (1.0 - BETA_TWO) / CORRECT_TWO

EXP = 128
TOK = 128
TOP = 6
CAP = 9
ROWS = EXP * CAP
MAIN = EXP * 8
HID = 768
HPART = 192
COLS = 640
WIDE = 768
PROWS = ROWS * HPART // 128
NONE = 99.0
LEG = (7, 2, 128)
MOVES = 8
STEP = 256
HALF = ROWS // 2
F32 = jnp.float32
BF16 = jnp.bfloat16

NN = (((1,), (0,)), ((), ()))
NT = (((1,), (1,)), ((), ()))


def params(limit=16):
    return pltpu.CompilerParams(vmem_limit_bytes=limit * 1024 * 1024)


def iota(shape, dim):
    return lax.broadcasted_iota(jnp.int32, shape, dim)


def mm(a, b, dims=NN):
    return lax.dot_general(a, b, dims, preferred_element_type=F32)


def thirds(x):
    high = x.astype(BF16)
    rest = x - high.astype(F32)
    mid = rest.astype(BF16)
    low = (rest - mid.astype(F32)).astype(BF16)
    return high, mid, low


def routed(route, gates, plan):
    diag = iota((EXP, EXP), 0) == iota((EXP, EXP), 1)
    column = jnp.sum(jnp.where(diag, plan.astype(F32), 0.0), axis=1, keepdims=True)
    named = route.astype(F32)
    member = jnp.zeros((EXP, TOK), F32)
    gate = jnp.zeros((EXP, TOK), F32)
    for k in range(TOP):
        same = named[k : k + 1, :] == column
        member = jnp.where(same, 1.0, member)
        gate = jnp.where(same, gates[k : k + 1, :], gate)
    earlier = (iota((TOK, TOK), 0) < iota((TOK, TOK), 1)).astype(F32).astype(BF16)
    rank = mm(member.astype(BF16), earlier)
    return jnp.where(member > 0.0, rank, NONE), gate


def onehot(mask):
    return jnp.where(mask, 1.0, 0.0).astype(BF16)


def main_pick(block):
    r = iota((128, 256), 0)
    return onehot(iota((128, 256), 1) == 16 * block + (r // 8) * 9 + r % 8)


def last_pick():
    return onehot(iota((EXP, ROWS), 1) == iota((EXP, ROWS), 0) * 9 + 8)


def prepare_second(h_ref, out_ref):
    for b in range(8):
        win = slice(128 * b, 128 * b + 256)
        out_ref[128 * b : 128 * b + 128, :] = mm(main_pick(b), h_ref[:, win], NT).astype(BF16)
    out_ref[MAIN:ROWS, :] = mm(last_pick(), h_ref[...], NT).astype(BF16)


def prepare_first(h_ref, out_ref):
    for b in range(8):
        win = slice(128 * b, 128 * b + 256)
        out_ref[:, 128 * b : 128 * b + 128] = mm(h_ref[:, win], main_pick(b), NT).astype(BF16)
    out_ref[:, MAIN:ROWS] = mm(h_ref[...], last_pick(), NT).astype(BF16)


def build_rows(route_ref, gates_ref, plan_ref, tokens_ref, out_ref, extra):
    rank, gate = routed(route_ref[...], gates_ref[...], plan_ref[...])
    tokens = tokens_ref[...]
    high, mid, low = thirds(gate)
    code = rank.astype(BF16)
    for b in range(4):
        r = iota((256, EXP), 0)
        spread = onehot(iota((256, EXP), 1) == 32 * b + r // 8)
        here = mm(spread, code) == (r % 8).astype(F32)
        gates_here = (mm(spread, high) + mm(spread, mid)) + mm(spread, low)
        scale = jnp.sum(jnp.where(here, gates_here, 0.0), axis=1, keepdims=True)
        rows = mm(onehot(here), tokens)
        out_ref[256 * b : 256 * b + 256, 0:COLS] = (scale * rows).astype(BF16)
    here = rank == 8.0
    scale = jnp.sum(jnp.where(here, gate, 0.0), axis=1, keepdims=True)
    rows = (scale * mm(onehot(here), tokens)).astype(BF16).astype(F32)
    extra[...] = jnp.zeros_like(extra)
    for q in range(5):
        extra[pl.ds(q, EXP, stride=8), :] = rows[:, 128 * q : 128 * q + 128]
    out_ref[:, COLS:WIDE] = extra[...].astype(BF16)


def choose(moves_ref, in_ref, out_ref):
    out_ref[...] = in_ref[...]
    for m in range(MOVES):
        out_ref[moves_ref[m]] = in_ref[moves_ref[MOVES + m]]


def last_rows(payload_ref, extra):
    extra[...] = payload_ref[:, COLS:WIDE].astype(F32)
    return jnp.concatenate(
        [extra[pl.ds(q, EXP, stride=8), :] for q in range(5)], axis=1
    ).astype(BF16)


def finish(
    payload_ref, one, two, first_hbm, master_hbm, second_hbm, out_hbm,
    first, master, second, weight, rows, extra, out, sems,
):
    steps = HID // STEP
    copies = []
    for n in range(steps):
        at = pl.ds(n * STEP, STEP)
        for i, (source, target) in enumerate(((first_hbm, first), (master_hbm, master))):
            copies.append(
                pltpu.make_async_copy(source.at[at], target.at[at], sems.at[2 * n + i])
            )
    copies.append(pltpu.make_async_copy(second_hbm, second, sems.at[2 * steps]))
    for copy in copies:
        copy.start()

    rows[0:MAIN, :] = payload_ref[:, 0:COLS]
    rows[MAIN:ROWS, :] = last_rows(payload_ref, extra)
    for n in range(steps):
        at = slice(n * STEP, n * STEP + STEP)
        copies[2 * n].wait()
        gradient = mm(first[at, :], rows[...])
        copies[2 * n + 1].wait()
        moment_new = ONE_OLD * one[at].astype(F32) + ONE_NEW * gradient
        moment_two = TWO_OLD * two[at].astype(F32) + TWO_NEW * gradient * gradient
        root = moment_two * lax.rsqrt(moment_two)
        updated = KEEP * master[at] - moment_new * pl.reciprocal(root + EPSILON)
        weight[at, :] = updated.astype(BF16)
    copies[-1].wait()

    extra[...] = jnp.zeros_like(extra)
    sent = []
    for n, (start, stop) in enumerate(((0, 256), (256, 512), (512, 640))):
        total = mm(second[...], weight[:, start:stop]).astype(BF16)
        out[:, start:stop] = total[0:MAIN]
        ends = total[MAIN:ROWS].astype(F32)
        for q in range(start // 128, stop // 128):
            at = 128 * q - start
            extra[pl.ds(q, EXP, stride=8), :] = ends[:, at : at + 128]
        if stop == COLS:
            out[:, COLS:WIDE] = extra[...].astype(BF16)
            stop = WIDE
        cols = pl.ds(start, stop - start)
        sent.append(
            pltpu.make_async_copy(
                out.at[:, cols], out_hbm.at[:, cols], sems.at[2 * steps + 1 + n]
            )
        )
        sent[-1].start()
    for copy in sent:
        copy.wait()


def mixing(route_ref, gates_ref, plan_ref, main_ref, last_ref):
    rank, gate = routed(route_ref[...], gates_ref[...], plan_ref[...])
    rank = rank.T
    gate = gate.T
    code = rank.astype(BF16)
    parts = thirds(gate)
    for b in range(4):
        c = iota((EXP, 256), 1)
        spread = onehot(iota((EXP, 256), 0) == 32 * b + c // 8)
        here = mm(code, spread) == (c % 8).astype(F32)
        for n, part in enumerate(parts):
            main_ref[128 * n : 128 * n + 128, 256 * b : 256 * b + 256] = jnp.where(
                here, mm(part, spread), 0.0
            ).astype(BF16)
    for n, part in enumerate(parts):
        last_ref[128 * n : 128 * n + 128, :] = jnp.where(
            rank == 8.0, part.astype(F32), 0.0
        ).astype(BF16)


def combine(main_ref, last_ref, payload_ref, out_ref, extra):
    total = mm(main_ref[...], payload_ref[:, 0:COLS]) + mm(
        last_ref[...], last_rows(payload_ref, extra)
    )
    out_ref[...] = (total[0:128] + (total[128:256] + total[256:384])).astype(BF16)


def shape(*extents, dtype=BF16):
    return jax.ShapeDtypeStruct(extents, dtype)


def exchange(x):
    return lax.all_to_all(x, "expert", split_axis=0, concat_axis=0, tiled=True)


def shards(
    cotangent,
    route_first,
    gates_first,
    hidden_first,
    route_second,
    gates_second,
    hidden_second,
    master,
    moment_one,
    moment_two,
    old_plan,
    new_plan,
):
    labels = jnp.arange(EXP, dtype=jnp.int32)
    plan = old_plan.reshape(1, EXP)
    moved = old_plan != new_plan
    order = jnp.sum(jnp.where((labels[None, :] < labels[:, None]) & moved[None, :], 1, 0), axis=1)
    chosen = (order[None, :] == labels[:MOVES, None]) & moved[None, :]
    to = jnp.sum(jnp.where(chosen, labels[None, :], 0), axis=1)
    source = jnp.sum(jnp.where(new_plan[None, :] == old_plan[:, None], labels[None, :], 0), axis=1)
    origin = jnp.sum(jnp.where(labels[None, :] == to[:, None], source[None, :], 0), axis=1)
    moves = jnp.concatenate([to, origin])
    extra = pltpu.VMEM((MAIN, 128), F32)
    hbm = pl.BlockSpec(memory_space=pltpu.HBM)
    smem = pl.BlockSpec(memory_space=pltpu.SMEM)
    vmem = pl.BlockSpec(memory_space=pltpu.VMEM)

    with jax.named_scope("second_hidden_out"):
        tiles = hidden_second[0].T.reshape(24, 8, 9, 128).transpose(0, 2, 1, 3)
        tiles = jnp.pad(tiles.reshape(PROWS, 128), ((0, EXP * 14 - PROWS), (0, 0)))
        spread = exchange(tiles.reshape(EXP, *LEG))

    with jax.named_scope("dispatch"):
        rows = pl.pallas_call(
            build_rows,
            out_shape=shape(MAIN, WIDE),
            scratch_shapes=[extra],
            compiler_params=params(),
        )(route_first.T, gates_first.T, plan, cotangent)
    with jax.named_scope("second_hidden_in"):
        kept = pl.pallas_call(
            choose,
            out_shape=shape(EXP, *LEG),
            in_specs=[smem, vmem],
            compiler_params=params(),
        )(moves, spread)
        kept, rows = lax.optimization_barrier((kept, rows))
        mine = exchange(kept).reshape(EXP * 14, 128)[:PROWS]
        mine = mine.reshape(24, 9, 8, 128).transpose(0, 2, 1, 3).reshape(HPART, ROWS)
        second = lax.all_gather(mine, "tensor", axis=0, tiled=True)
        second = pl.pallas_call(
            prepare_second, out_shape=shape(ROWS, HID), compiler_params=params(), cost_estimate=pl.CostEstimate(flops=10*1000*1000000, bytes_accessed=0, transcendentals=0)
        )(second)

    with jax.named_scope("dispatch"):
        arrived = exchange(rows.reshape(EXP, 8, WIDE)).reshape(MAIN, WIDE)

    with jax.named_scope("first_hidden"):
        first = lax.all_gather(hidden_first[0].T, "tensor", axis=0, tiled=True)
        first = pl.pallas_call(
            prepare_first, out_shape=shape(HID, ROWS), compiler_params=params()
        )(first)

    with jax.named_scope("mixing"):
        mix, mix_last = pl.pallas_call(
            mixing,
            out_shape=(shape(3 * TOK, MAIN), shape(3 * TOK, EXP)),
            compiler_params=params(),
        )(route_second.T, gates_second.T, plan)

    with jax.named_scope("finish"):
        produced = pl.pallas_call(
            finish,
            in_specs=[vmem, vmem, vmem, hbm, hbm, hbm],
            out_specs=hbm,
            out_shape=shape(MAIN, WIDE),
            scratch_shapes=[
                pltpu.VMEM((HID, ROWS), BF16),
                pltpu.VMEM((HID, COLS), F32),
                pltpu.VMEM((ROWS, HID), BF16),
                pltpu.VMEM((HID, COLS), BF16),
                pltpu.VMEM((ROWS, COLS), BF16),
                extra,
                pltpu.VMEM((MAIN, WIDE), BF16),
                pltpu.SemaphoreType.DMA((2 * (HID // STEP) + 4,)),
            ],
            compiler_params=params(48),
        )(arrived, moment_one[0], moment_two[0], first, master[0], second)
        returned = exchange(produced.reshape(EXP, 8, WIDE)).reshape(MAIN, WIDE)

    with jax.named_scope("combine"):
        return pl.pallas_call(
            combine,
            out_shape=shape(TOK, COLS),
            scratch_shapes=[extra],
            compiler_params=params(),
        )(mix, mix_last, returned)


def solution(mesh):
    placed = (
        P("expert", "tensor"),
        P("expert", None),
        P("expert", None),
        P("expert", None, "tensor"),
        P("expert", None),
        P("expert", None),
        P("expert", None, "tensor"),
        P("expert", None, "tensor"),
        P("expert", None, "tensor"),
        P("expert", None, "tensor"),
        P(),
        P(),
    )
    return jax.shard_map(
        shards, mesh=mesh, in_specs=placed, out_specs=P("expert", "tensor"), check_vma=False
    )
```

```python
import jax
import jax.numpy as jnp
from jax import lax
from jax.experimental import pallas as pl
from jax.experimental.pallas import tpu as pltpu
from jax.sharding import PartitionSpec as P

BETA_ONE = 0.9
BETA_TWO = 0.95
CORRECT_ONE = 1.0 - 0.9**10
CORRECT_TWO = 1.0 - 0.95**10
LEARN_RATE = 0.04
WEIGHT_DECAY = 0.1
EPSILON = 1e-08
KEEP = 1.0 - LEARN_RATE * WEIGHT_DECAY
ONE_OLD = LEARN_RATE * BETA_ONE / CORRECT_ONE
ONE_NEW = LEARN_RATE * (1.0 - BETA_ONE) / CORRECT_ONE
TWO_OLD = BETA_TWO / CORRECT_TWO
TWO_NEW = (1.0 - BETA_TWO) / CORRECT_TWO

EXP = 128
TOK = 128
TOP = 6
CAP = 9
ROWS = EXP * CAP
MAIN = EXP * 8
HID = 768
HPART = 192
COLS = 640
WIDE = 768
PROWS = ROWS * HPART // 128
NONE = 99.0
LEG = (7, 2, 128)
MOVES = 8
F32 = jnp.float32
BF16 = jnp.bfloat16

NN = (((1,), (0,)), ((), ()))
NT = (((1,), (1,)), ((), ()))


def params(limit=16):
    return pltpu.CompilerParams(vmem_limit_bytes=limit * 1024 * 1024)


def iota(shape, dim):
    return lax.broadcasted_iota(jnp.int32, shape, dim)


def mm(a, b, dims=NN):
    return lax.dot_general(a, b, dims, preferred_element_type=F32)


def thirds(x):
    high = x.astype(BF16)
    rest = x - high.astype(F32)
    mid = rest.astype(BF16)
    low = (rest - mid.astype(F32)).astype(BF16)
    return high, mid, low


def routed(route, gates, plan):
    diag = iota((EXP, EXP), 0) == iota((EXP, EXP), 1)
    column = jnp.sum(jnp.where(diag, plan.astype(F32), 0.0), axis=1, keepdims=True)
    named = route.astype(F32)
    member = jnp.zeros((EXP, TOK), F32)
    gate = jnp.zeros((EXP, TOK), F32)
    for k in range(TOP):
        same = named[k : k + 1, :] == column
        member = jnp.where(same, 1.0, member)
        gate = jnp.where(same, gates[k : k + 1, :], gate)
    earlier = (iota((TOK, TOK), 0) < iota((TOK, TOK), 1)).astype(F32).astype(BF16)
    rank = mm(member.astype(BF16), earlier)
    return jnp.where(member > 0.0, rank, NONE), gate


def onehot(mask):
    return jnp.where(mask, 1.0, 0.0).astype(BF16)


def main_pick(block):
    r = iota((128, 256), 0)
    return onehot(iota((128, 256), 1) == 16 * block + (r // 8) * 9 + r % 8)


def last_pick():
    return onehot(iota((EXP, ROWS), 1) == iota((EXP, ROWS), 0) * 9 + 8)


def prepare_second(zero_ref, one_ref, two_ref, three_ref, out_ref):
    parts = [ref[...] for ref in (zero_ref, one_ref, two_ref, three_ref)]
    whole = jnp.concatenate(parts, axis=0)
    for b in range(8):
        win = slice(128 * b, 128 * b + 256)
        out_ref[128 * b : 128 * b + 128, :] = mm(main_pick(b), whole[:, win], NT).astype(BF16)
    out_ref[MAIN:ROWS, :] = mm(last_pick(), whole, NT).astype(BF16)


def prepare_first(zero_ref, one_ref, two_ref, three_ref, out_ref):
    for n, ref in enumerate((zero_ref, one_ref, two_ref, three_ref)):
        at = slice(n * HPART, n * HPART + HPART)
        for b in range(8):
            win = slice(128 * b, 128 * b + 256)
            out_ref[at, 128 * b : 128 * b + 128] = mm(ref[:, win], main_pick(b), NT).astype(BF16)
        out_ref[at, MAIN:ROWS] = mm(ref[...], last_pick(), NT).astype(BF16)


def build_rows(route_ref, gates_ref, plan_ref, tokens_ref, out_ref, extra):
    rank, gate = routed(route_ref[...], gates_ref[...], plan_ref[...])
    tokens = tokens_ref[...]
    high, mid, low = thirds(gate)
    code = rank.astype(BF16)
    for b in range(4):
        r = iota((256, EXP), 0)
        spread = onehot(iota((256, EXP), 1) == 32 * b + r // 8)
        here = mm(spread, code) == (r % 8).astype(F32)
        gates_here = (mm(spread, high) + mm(spread, mid)) + mm(spread, low)
        scale = jnp.sum(jnp.where(here, gates_here, 0.0), axis=1, keepdims=True)
        rows = mm(onehot(here), tokens)
        out_ref[256 * b : 256 * b + 256, 0:COLS] = (scale * rows).astype(BF16)
    here = rank == 8.0
    scale = jnp.sum(jnp.where(here, gate, 0.0), axis=1, keepdims=True)
    rows = (scale * mm(onehot(here), tokens)).astype(BF16).astype(F32)
    extra[...] = jnp.zeros_like(extra)
    for q in range(5):
        extra[pl.ds(q, EXP, stride=8), :] = rows[:, 128 * q : 128 * q + 128]
    out_ref[:, COLS:WIDE] = extra[...].astype(BF16)


def choose(moves_ref, in_ref, out_ref):
    out_ref[...] = in_ref[...]
    for m in range(MOVES):
        out_ref[moves_ref[m]] = in_ref[moves_ref[MOVES + m]]


def last_rows(payload_ref, extra):
    extra[...] = payload_ref[:, COLS:WIDE].astype(F32)
    return jnp.concatenate(
        [extra[pl.ds(q, EXP, stride=8), :] for q in range(5)], axis=1
    ).astype(BF16)


def finish(
    payload_ref, one, two, first_hbm, master_hbm, second_hbm, out_hbm,
    first, master, second, weight, rows, extra, out, sems,
):
    me = lax.axis_index("tensor")
    copies, places = [], []
    for n in range(4):
        at = pl.ds(n * HPART, HPART)
        place = pl.ds(pl.multiple_of(lax.rem(me + 4 - n, 4) * HPART, HPART), HPART)
        places.append(place)
        copies.append(pltpu.make_async_copy(first_hbm.at[at], first.at[at], sems.at[2 * n]))
        copies.append(
            pltpu.make_async_copy(master_hbm.at[place], master.at[at], sems.at[2 * n + 1])
        )
    copies.append(pltpu.make_async_copy(second_hbm, second, sems.at[8]))
    for copy in copies:
        copy.start()

    rows[0:MAIN, :] = payload_ref[:, 0:COLS]
    rows[MAIN:ROWS, :] = last_rows(payload_ref, extra)
    for n in range(4):
        at = slice(n * HPART, n * HPART + HPART)
        copies[2 * n].wait()
        gradient = mm(first[at, :], rows[...])
        copies[2 * n + 1].wait()
        moment_new = ONE_OLD * one[places[n], :].astype(F32) + ONE_NEW * gradient
        moment_two = TWO_OLD * two[places[n], :].astype(F32) + TWO_NEW * gradient * gradient
        root = moment_two * lax.rsqrt(moment_two)
        updated = KEEP * master[at, :] - moment_new * pl.reciprocal(root + EPSILON)
        weight[at, :] = updated.astype(BF16)
    copies[-1].wait()

    extra[...] = jnp.zeros_like(extra)
    sent = []
    for n, (start, stop) in enumerate(((0, 256), (256, 512), (512, 640))):
        total = mm(second[...], weight[:, start:stop]).astype(BF16)
        out[:, start:stop] = total[0:MAIN]
        ends = total[MAIN:ROWS].astype(F32)
        for q in range(start // 128, stop // 128):
            at = 128 * q - start
            extra[pl.ds(q, EXP, stride=8), :] = ends[:, at : at + 128]
        if stop == COLS:
            out[:, COLS:WIDE] = extra[...].astype(BF16)
            stop = WIDE
        cols = pl.ds(start, stop - start)
        sent.append(
            pltpu.make_async_copy(
                out.at[:, cols], out_hbm.at[:, cols], sems.at[9 + n]
            )
        )
        sent[-1].start()
    for copy in sent:
        copy.wait()


def mixing(route_ref, gates_ref, plan_ref, main_ref, last_ref):
    rank, gate = routed(route_ref[...], gates_ref[...], plan_ref[...])
    rank = rank.T
    gate = gate.T
    code = rank.astype(BF16)
    parts = thirds(gate)
    for b in range(4):
        c = iota((EXP, 256), 1)
        spread = onehot(iota((EXP, 256), 0) == 32 * b + c // 8)
        here = mm(code, spread) == (c % 8).astype(F32)
        for n, part in enumerate(parts):
            main_ref[128 * n : 128 * n + 128, 256 * b : 256 * b + 256] = jnp.where(
                here, mm(part, spread), 0.0
            ).astype(BF16)
    for n, part in enumerate(parts):
        last_ref[128 * n : 128 * n + 128, :] = jnp.where(
            rank == 8.0, part.astype(F32), 0.0
        ).astype(BF16)


def combine(main_ref, last_ref, payload_ref, out_ref, extra):
    total = mm(main_ref[...], payload_ref[:, 0:COLS]) + mm(
        last_ref[...], last_rows(payload_ref, extra)
    )
    out_ref[...] = (total[0:128] + (total[128:256] + total[256:384])).astype(BF16)


def shape(*extents, dtype=BF16):
    return jax.ShapeDtypeStruct(extents, dtype)


def exchange(x):
    return lax.all_to_all(x, "expert", split_axis=0, concat_axis=0, tiled=True)


def before(x, shift):
    return lax.ppermute(x, "tensor", [(i, (i + shift) % 4) for i in range(4)])


def gather(x):
    return [x] + [before(x, shift) for shift in (1, 2, 3)]


def shards(
    cotangent,
    route_first,
    gates_first,
    hidden_first,
    route_second,
    gates_second,
    hidden_second,
    master,
    moment_one,
    moment_two,
    old_plan,
    new_plan,
):
    labels = jnp.arange(EXP, dtype=jnp.int32)
    plan = old_plan.reshape(1, EXP)
    moved = old_plan != new_plan
    order = jnp.sum(jnp.where((labels[None, :] < labels[:, None]) & moved[None, :], 1, 0), axis=1)
    chosen = (order[None, :] == labels[:MOVES, None]) & moved[None, :]
    to = jnp.sum(jnp.where(chosen, labels[None, :], 0), axis=1)
    source = jnp.sum(jnp.where(new_plan[None, :] == old_plan[:, None], labels[None, :], 0), axis=1)
    origin = jnp.sum(jnp.where(labels[None, :] == to[:, None], source[None, :], 0), axis=1)
    moves = jnp.concatenate([to, origin])
    extra = pltpu.VMEM((MAIN, 128), F32)
    hbm = pl.BlockSpec(memory_space=pltpu.HBM)
    smem = pl.BlockSpec(memory_space=pltpu.SMEM)
    vmem = pl.BlockSpec(memory_space=pltpu.VMEM)

    with jax.named_scope("second_hidden_out"):
        tiles = hidden_second[0].T.reshape(24, 8, 9, 128).transpose(0, 2, 1, 3)
        tiles = jnp.pad(tiles.reshape(PROWS, 128), ((0, EXP * 14 - PROWS), (0, 0)))
        spread = exchange(tiles.reshape(EXP, *LEG))

    with jax.named_scope("dispatch"):
        rows = pl.pallas_call(
            build_rows,
            out_shape=shape(MAIN, WIDE),
            scratch_shapes=[extra],
            compiler_params=params(),
        )(route_first.T, gates_first.T, plan, cotangent)
    with jax.named_scope("second_hidden_in"):
        kept = pl.pallas_call(
            choose,
            out_shape=shape(EXP, *LEG),
            in_specs=[smem, vmem],
            compiler_params=params(),
        )(moves, spread)
        part = hidden_first[0].T
        near, far = before(part, 1), before(part, 3)
        kept, rows, near, far = lax.optimization_barrier((kept, rows, near, far))
        second = [
            piece.reshape(EXP * 14, 128)[:PROWS]
            .reshape(24, 9, 8, 128)
            .transpose(0, 2, 1, 3)
            .reshape(HPART, ROWS)
            for piece in gather(exchange(kept))
        ]
        second = pl.pallas_call(
            prepare_second, out_shape=shape(ROWS, HID), compiler_params=params()
        )(*second)

    with jax.named_scope("dispatch"):
        rows, across = lax.optimization_barrier((rows, before(part, 2)))
        arrived = exchange(rows.reshape(EXP, 8, WIDE)).reshape(MAIN, WIDE)

    with jax.named_scope("first_hidden"):
        first = pl.pallas_call(
            prepare_first, out_shape=shape(HID, ROWS), compiler_params=params()
        )(part, near, across, far)

    with jax.named_scope("mixing"):
        mix, mix_last = pl.pallas_call(
            mixing,
            out_shape=(shape(3 * TOK, MAIN), shape(3 * TOK, EXP)),
            compiler_params=params(),
        )(route_second.T, gates_second.T, plan)

    with jax.named_scope("finish"):
        produced = pl.pallas_call(
            finish,
            in_specs=[vmem, vmem, vmem, hbm, hbm, hbm],
            out_specs=hbm,
            out_shape=shape(MAIN, WIDE),
            scratch_shapes=[
                pltpu.VMEM((HID, ROWS), BF16),
                pltpu.VMEM((HID, COLS), F32),
                pltpu.VMEM((ROWS, HID), BF16),
                pltpu.VMEM((HID, COLS), BF16),
                pltpu.VMEM((ROWS, COLS), BF16),
                extra,
                pltpu.VMEM((MAIN, WIDE), BF16),
                pltpu.SemaphoreType.DMA((12,)),
            ],
            compiler_params=params(48),
        )(arrived, moment_one[0], moment_two[0], first, master[0], second)
        returned = exchange(produced.reshape(EXP, 8, WIDE)).reshape(MAIN, WIDE)

    with jax.named_scope("combine"):
        return pl.pallas_call(
            combine,
            out_shape=shape(TOK, COLS),
            scratch_shapes=[extra],
            compiler_params=params(),
        )(mix, mix_last, returned)


def solution(mesh):
    placed = (
        P("expert", "tensor"),
        P("expert", None),
        P("expert", None),
        P("expert", None, "tensor"),
        P("expert", None),
        P("expert", None),
        P("expert", None, "tensor"),
        P("expert", None, "tensor"),
        P("expert", None, "tensor"),
        P("expert", None, "tensor"),
        P(),
        P(),
    )
    return jax.shard_map(
        shards, mesh=mesh, in_specs=placed, out_specs=P("expert", "tensor"), check_vma=False
    )
```

```python
import jax
import jax.numpy as jnp
from jax import lax
from jax.experimental import pallas as pl
from jax.experimental.pallas import tpu as pltpu
from jax.sharding import PartitionSpec as P

BETA_ONE = 0.9
BETA_TWO = 0.95
CORRECT_ONE = 1.0 - 0.9**10
CORRECT_TWO = 1.0 - 0.95**10
LEARN_RATE = 0.04
WEIGHT_DECAY = 0.1
EPSILON = 1e-08
KEEP = 1.0 - LEARN_RATE * WEIGHT_DECAY
ONE_OLD = LEARN_RATE * BETA_ONE / CORRECT_ONE
ONE_NEW = LEARN_RATE * (1.0 - BETA_ONE) / CORRECT_ONE
TWO_OLD = BETA_TWO / CORRECT_TWO
TWO_NEW = (1.0 - BETA_TWO) / CORRECT_TWO

EXP = 128
TOK = 128
TOP = 6
CAP = 9
ROWS = EXP * CAP
MAIN = EXP * 8
HID = 768
HPART = 192
COLS = 640
WIDE = 768
PROWS = ROWS * HPART // 128
NONE = 99.0
LEG = (7, 2, 128)
MOVES = 8
F32 = jnp.float32
BF16 = jnp.bfloat16

NN = (((1,), (0,)), ((), ()))
NT = (((1,), (1,)), ((), ()))


def params(limit=16):
    return pltpu.CompilerParams(vmem_limit_bytes=limit * 1024 * 1024)


def iota(shape, dim):
    return lax.broadcasted_iota(jnp.int32, shape, dim)


def mm(a, b, dims=NN):
    return lax.dot_general(a, b, dims, preferred_element_type=F32)


def thirds(x):
    high = x.astype(BF16)
    rest = x - high.astype(F32)
    mid = rest.astype(BF16)
    low = (rest - mid.astype(F32)).astype(BF16)
    return high, mid, low


def routed(route, gates, plan):
    diag = iota((EXP, EXP), 0) == iota((EXP, EXP), 1)
    column = jnp.sum(jnp.where(diag, plan.astype(F32), 0.0), axis=1, keepdims=True)
    named = route.astype(F32)
    member = jnp.zeros((EXP, TOK), F32)
    gate = jnp.zeros((EXP, TOK), F32)
    for k in range(TOP):
        same = named[k : k + 1, :] == column
        member = jnp.where(same, 1.0, member)
        gate = jnp.where(same, gates[k : k + 1, :], gate)
    earlier = (iota((TOK, TOK), 0) < iota((TOK, TOK), 1)).astype(F32).astype(BF16)
    rank = mm(member.astype(BF16), earlier)
    return jnp.where(member > 0.0, rank, NONE), gate


def onehot(mask):
    return jnp.where(mask, 1.0, 0.0).astype(BF16)


def main_pick(block):
    r = iota((128, 256), 0)
    return onehot(iota((128, 256), 1) == 16 * block + (r // 8) * 9 + r % 8)


def last_pick():
    return onehot(iota((EXP, ROWS), 1) == iota((EXP, ROWS), 0) * 9 + 8)


def prepare_second(zero_ref, one_ref, two_ref, three_ref, out_ref):
    parts = [ref[...] for ref in (zero_ref, one_ref, two_ref, three_ref)]
    whole = jnp.concatenate(parts, axis=0)
    for b in range(8):
        win = slice(128 * b, 128 * b + 256)
        out_ref[128 * b : 128 * b + 128, :] = mm(main_pick(b), whole[:, win], NT).astype(BF16)
    out_ref[MAIN:ROWS, :] = mm(last_pick(), whole, NT).astype(BF16)


def prepare_first(zero_ref, one_ref, two_ref, three_ref, out_ref):
    for n, ref in enumerate((zero_ref, one_ref, two_ref, three_ref)):
        at = slice(n * HPART, n * HPART + HPART)
        for b in range(8):
            win = slice(128 * b, 128 * b + 256)
            out_ref[at, 128 * b : 128 * b + 128] = mm(ref[:, win], main_pick(b), NT).astype(BF16)
        out_ref[at, MAIN:ROWS] = mm(ref[...], last_pick(), NT).astype(BF16)


def build_rows(route_ref, gates_ref, plan_ref, tokens_ref, out_ref, extra):
    rank, gate = routed(route_ref[...], gates_ref[...], plan_ref[...])
    tokens = tokens_ref[...]
    high, mid, low = thirds(gate)
    code = rank.astype(BF16)
    for b in range(4):
        r = iota((256, EXP), 0)
        spread = onehot(iota((256, EXP), 1) == 32 * b + r // 8)
        here = mm(spread, code) == (r % 8).astype(F32)
        gates_here = (mm(spread, high) + mm(spread, mid)) + mm(spread, low)
        scale = jnp.sum(jnp.where(here, gates_here, 0.0), axis=1, keepdims=True)
        rows = mm(onehot(here), tokens)
        out_ref[256 * b : 256 * b + 256, 0:COLS] = (scale * rows).astype(BF16)
    here = rank == 8.0
    scale = jnp.sum(jnp.where(here, gate, 0.0), axis=1, keepdims=True)
    rows = (scale * mm(onehot(here), tokens)).astype(BF16).astype(F32)
    extra[...] = jnp.zeros_like(extra)
    for q in range(5):
        extra[pl.ds(q, EXP, stride=8), :] = rows[:, 128 * q : 128 * q + 128]
    out_ref[:, COLS:WIDE] = extra[...].astype(BF16)


def choose(moves_ref, in_ref, out_ref):
    out_ref[...] = in_ref[...]
    for m in range(MOVES):
        out_ref[moves_ref[m]] = in_ref[moves_ref[MOVES + m]]


def last_rows(payload_ref, extra):
    extra[...] = payload_ref[:, COLS:WIDE].astype(F32)
    return jnp.concatenate(
        [extra[pl.ds(q, EXP, stride=8), :] for q in range(5)], axis=1
    ).astype(BF16)


def finish(
    payload_ref, one, two, first_hbm, master_hbm, second_hbm, out_hbm,
    first, master, second, weight, rows, extra, out, sems,
):
    me = lax.axis_index("tensor")
    copies, places = [], []
    for n in range(4):
        at = pl.ds(n * HPART, HPART)
        place = pl.ds(pl.multiple_of(lax.rem(me + 4 - n, 4) * HPART, HPART), HPART)
        places.append(place)
        copies.append(pltpu.make_async_copy(first_hbm.at[at], first.at[at], sems.at[2 * n]))
        copies.append(
            pltpu.make_async_copy(master_hbm.at[place], master.at[at], sems.at[2 * n + 1])
        )
    copies.append(pltpu.make_async_copy(second_hbm, second, sems.at[8]))
    for copy in copies:
        copy.start()

    rows[0:MAIN, :] = payload_ref[:, 0:COLS]
    rows[MAIN:ROWS, :] = last_rows(payload_ref, extra)
    for n in range(4):
        at = slice(n * HPART, n * HPART + HPART)
        copies[2 * n].wait()
        gradient = mm(first[at, :], rows[...])
        copies[2 * n + 1].wait()
        moment_new = ONE_OLD * one[places[n], :].astype(F32) + ONE_NEW * gradient
        moment_two = TWO_OLD * two[places[n], :].astype(F32) + TWO_NEW * gradient * gradient
        root = moment_two * lax.rsqrt(moment_two)
        updated = KEEP * master[at, :] - moment_new * pl.reciprocal(root + EPSILON)
        weight[at, :] = updated.astype(BF16)
    copies[-1].wait()

    extra[...] = jnp.zeros_like(extra)
    sent = []
    for n, (start, stop) in enumerate(((0, 256), (256, 512), (512, 640))):
        total = mm(second[...], weight[:, start:stop]).astype(BF16)
        out[:, start:stop] = total[0:MAIN]
        ends = total[MAIN:ROWS].astype(F32)
        for q in range(start // 128, stop // 128):
            at = 128 * q - start
            extra[pl.ds(q, EXP, stride=8), :] = ends[:, at : at + 128]
        if stop == COLS:
            out[:, COLS:WIDE] = extra[...].astype(BF16)
            stop = WIDE
        cols = pl.ds(start, stop - start)
        sent.append(
            pltpu.make_async_copy(
                out.at[:, cols], out_hbm.at[:, cols], sems.at[9 + n]
            )
        )
        sent[-1].start()
    for copy in sent:
        copy.wait()


def mixing(route_ref, gates_ref, plan_ref, main_ref, last_ref):
    rank, gate = routed(route_ref[...], gates_ref[...], plan_ref[...])
    rank = rank.T
    gate = gate.T
    code = rank.astype(BF16)
    parts = thirds(gate)
    for b in range(4):
        c = iota((EXP, 256), 1)
        spread = onehot(iota((EXP, 256), 0) == 32 * b + c // 8)
        here = mm(code, spread) == (c % 8).astype(F32)
        for n, part in enumerate(parts):
            main_ref[128 * n : 128 * n + 128, 256 * b : 256 * b + 256] = jnp.where(
                here, mm(part, spread), 0.0
            ).astype(BF16)
    for n, part in enumerate(parts):
        last_ref[128 * n : 128 * n + 128, :] = jnp.where(
            rank == 8.0, part.astype(F32), 0.0
        ).astype(BF16)


def combine(main_ref, last_ref, payload_ref, out_ref, extra):
    total = mm(main_ref[...], payload_ref[:, 0:COLS]) + mm(
        last_ref[...], last_rows(payload_ref, extra)
    )
    out_ref[...] = (total[0:128] + (total[128:256] + total[256:384])).astype(BF16)


def shape(*extents, dtype=BF16):
    return jax.ShapeDtypeStruct(extents, dtype)


def exchange(x):
    return lax.all_to_all(x, "expert", split_axis=0, concat_axis=0, tiled=True)


def before(x, shift):
    return lax.ppermute(x, "tensor", [(i, (i + shift) % 4) for i in range(4)])


def gather(x):
    return [x] + [before(x, shift) for shift in (1, 2, 3)]


def shards(
    cotangent,
    route_first,
    gates_first,
    hidden_first,
    route_second,
    gates_second,
    hidden_second,
    master,
    moment_one,
    moment_two,
    old_plan,
    new_plan,
):
    labels = jnp.arange(EXP, dtype=jnp.int32)
    plan = old_plan.reshape(1, EXP)
    moved = old_plan != new_plan
    order = jnp.sum(jnp.where((labels[None, :] < labels[:, None]) & moved[None, :], 1, 0), axis=1)
    chosen = (order[None, :] == labels[:MOVES, None]) & moved[None, :]
    to = jnp.sum(jnp.where(chosen, labels[None, :], 0), axis=1)
    source = jnp.sum(jnp.where(new_plan[None, :] == old_plan[:, None], labels[None, :], 0), axis=1)
    origin = jnp.sum(jnp.where(labels[None, :] == to[:, None], source[None, :], 0), axis=1)
    moves = jnp.concatenate([to, origin])
    extra = pltpu.VMEM((MAIN, 128), F32)
    hbm = pl.BlockSpec(memory_space=pltpu.HBM)
    smem = pl.BlockSpec(memory_space=pltpu.SMEM)
    vmem = pl.BlockSpec(memory_space=pltpu.VMEM)

    with jax.named_scope("second_hidden_out"):
        tiles = hidden_second[0].T.reshape(24, 8, 9, 128).transpose(0, 2, 1, 3)
        tiles = jnp.pad(tiles.reshape(PROWS, 128), ((0, EXP * 14 - PROWS), (0, 0)))
        spread = exchange(tiles.reshape(EXP, *LEG))

    with jax.named_scope("dispatch"):
        rows = pl.pallas_call(
            build_rows,
            out_shape=shape(MAIN, WIDE),
            scratch_shapes=[extra],
            compiler_params=params(),
        )(route_first.T, gates_first.T, plan, cotangent)
    with jax.named_scope("second_hidden_in"):
        kept = pl.pallas_call(
            choose,
            out_shape=shape(EXP, *LEG),
            in_specs=[smem, vmem],
            compiler_params=params(),
        )(moves, spread)
        part = hidden_first[0].T
        near = before(part, 1)
        kept, rows, near = lax.optimization_barrier((kept, rows, near))
        second = [
            piece.reshape(EXP * 14, 128)[:PROWS]
            .reshape(24, 9, 8, 128)
            .transpose(0, 2, 1, 3)
            .reshape(HPART, ROWS)
            for piece in gather(exchange(kept))
        ]
        second = pl.pallas_call(
            prepare_second, out_shape=shape(ROWS, HID), compiler_params=params()
        )(*second)

    with jax.named_scope("dispatch"):
        rows, across, far = lax.optimization_barrier((rows, before(near, 1), before(part, 3)))
        arrived = exchange(rows.reshape(EXP, 8, WIDE)).reshape(MAIN, WIDE)

    with jax.named_scope("first_hidden"):
        first = pl.pallas_call(
            prepare_first, out_shape=shape(HID, ROWS), compiler_params=params()
        )(part, near, across, far)

    with jax.named_scope("mixing"):
        mix, mix_last = pl.pallas_call(
            mixing,
            out_shape=(shape(3 * TOK, MAIN), shape(3 * TOK, EXP)),
            compiler_params=params(),
        )(route_second.T, gates_second.T, plan)

    with jax.named_scope("finish"):
        produced = pl.pallas_call(
            finish,
            in_specs=[vmem, vmem, vmem, hbm, hbm, hbm],
            out_specs=hbm,
            out_shape=shape(MAIN, WIDE),
            scratch_shapes=[
                pltpu.VMEM((HID, ROWS), BF16),
                pltpu.VMEM((HID, COLS), F32),
                pltpu.VMEM((ROWS, HID), BF16),
                pltpu.VMEM((HID, COLS), BF16),
                pltpu.VMEM((ROWS, COLS), BF16),
                extra,
                pltpu.VMEM((MAIN, WIDE), BF16),
                pltpu.SemaphoreType.DMA((12,)),
            ],
            compiler_params=params(48),
        )(arrived, moment_one[0], moment_two[0], first, master[0], second)
        returned = exchange(produced.reshape(EXP, 8, WIDE)).reshape(MAIN, WIDE)

    with jax.named_scope("combine"):
        return pl.pallas_call(
            combine,
            out_shape=shape(TOK, COLS),
            scratch_shapes=[extra],
            compiler_params=params(),
        )(mix, mix_last, returned)


def solution(mesh):
    placed = (
        P("expert", "tensor"),
        P("expert", None),
        P("expert", None),
        P("expert", None, "tensor"),
        P("expert", None),
        P("expert", None),
        P("expert", None, "tensor"),
        P("expert", None, "tensor"),
        P("expert", None, "tensor"),
        P("expert", None, "tensor"),
        P(),
        P(),
    )
    return jax.shard_map(
        shards, mesh=mesh, in_specs=placed, out_specs=P("expert", "tensor"), check_vma=False
    )
```

```python
import jax
import jax.numpy as jnp
from jax import lax
from jax.experimental import pallas as pl
from jax.experimental.pallas import tpu as pltpu
from jax.sharding import PartitionSpec as P

BETA_ONE = 0.9
BETA_TWO = 0.95
CORRECT_ONE = 1.0 - 0.9**10
CORRECT_TWO = 1.0 - 0.95**10
LEARN_RATE = 0.04
WEIGHT_DECAY = 0.1
EPSILON = 1e-08
KEEP = 1.0 - LEARN_RATE * WEIGHT_DECAY
ONE_OLD = LEARN_RATE * BETA_ONE / CORRECT_ONE
ONE_NEW = LEARN_RATE * (1.0 - BETA_ONE) / CORRECT_ONE
TWO_OLD = BETA_TWO / CORRECT_TWO
TWO_NEW = (1.0 - BETA_TWO) / CORRECT_TWO

EXP = 128
TOK = 128
TOP = 6
CAP = 9
ROWS = EXP * CAP
MAIN = EXP * 8
HID = 768
HPART = 192
COLS = 640
WIDE = 768
PROWS = ROWS * HPART // 128
NONE = 99.0
LEG = (7, 2, 128)
MOVES = 8
F32 = jnp.float32
BF16 = jnp.bfloat16

NN = (((1,), (0,)), ((), ()))
NT = (((1,), (1,)), ((), ()))


def params(limit=16):
    return pltpu.CompilerParams(vmem_limit_bytes=limit * 1024 * 1024)


def iota(shape, dim):
    return lax.broadcasted_iota(jnp.int32, shape, dim)


def mm(a, b, dims=NN):
    return lax.dot_general(a, b, dims, preferred_element_type=F32)


def thirds(x):
    high = x.astype(BF16)
    rest = x - high.astype(F32)
    mid = rest.astype(BF16)
    low = (rest - mid.astype(F32)).astype(BF16)
    return high, mid, low


def routed(route, gates, plan):
    diag = iota((EXP, EXP), 0) == iota((EXP, EXP), 1)
    column = jnp.sum(jnp.where(diag, plan.astype(F32), 0.0), axis=1, keepdims=True)
    named = route.astype(F32)
    member = jnp.zeros((EXP, TOK), F32)
    gate = jnp.zeros((EXP, TOK), F32)
    for k in range(TOP):
        same = named[k : k + 1, :] == column
        member = jnp.where(same, 1.0, member)
        gate = jnp.where(same, gates[k : k + 1, :], gate)
    earlier = (iota((TOK, TOK), 0) < iota((TOK, TOK), 1)).astype(F32).astype(BF16)
    rank = mm(member.astype(BF16), earlier)
    return jnp.where(member > 0.0, rank, NONE), gate


def onehot(mask):
    return jnp.where(mask, 1.0, 0.0).astype(BF16)


def main_pick(block):
    r = iota((128, 256), 0)
    return onehot(iota((128, 256), 1) == 16 * block + (r // 8) * 9 + r % 8)


def last_pick():
    return onehot(iota((EXP, ROWS), 1) == iota((EXP, ROWS), 0) * 9 + 8)


def prepare_second(zero_ref, one_ref, three_ref, two_low_ref, two_high_ref, out_ref):
    refs = (zero_ref, one_ref, three_ref, two_low_ref, two_high_ref)
    whole = jnp.concatenate([ref[...] for ref in refs], axis=0)
    for b in range(8):
        win = slice(128 * b, 128 * b + 256)
        out_ref[128 * b : 128 * b + 128, :] = mm(main_pick(b), whole[:, win], NT).astype(BF16)
    out_ref[MAIN:ROWS, :] = mm(last_pick(), whole, NT).astype(BF16)


def prepare_first(zero_ref, one_ref, three_ref, two_low_ref, two_high_ref, out_ref):
    at = 0
    for ref in (zero_ref, one_ref, three_ref, two_low_ref, two_high_ref):
        to = at + ref.shape[0]
        for b in range(8):
            win = slice(128 * b, 128 * b + 256)
            picked = mm(ref[:, win], main_pick(b), NT).astype(BF16)
            out_ref[at:to, 128 * b : 128 * b + 128] = picked
        out_ref[at:to, MAIN:ROWS] = mm(ref[...], last_pick(), NT).astype(BF16)
        at = to


def build_rows(route_ref, gates_ref, plan_ref, tokens_ref, out_ref, extra):
    rank, gate = routed(route_ref[...], gates_ref[...], plan_ref[...])
    tokens = tokens_ref[...]
    high, mid, low = thirds(gate)
    code = rank.astype(BF16)
    for b in range(4):
        r = iota((256, EXP), 0)
        spread = onehot(iota((256, EXP), 1) == 32 * b + r // 8)
        here = mm(spread, code) == (r % 8).astype(F32)
        gates_here = (mm(spread, high) + mm(spread, mid)) + mm(spread, low)
        scale = jnp.sum(jnp.where(here, gates_here, 0.0), axis=1, keepdims=True)
        rows = mm(onehot(here), tokens)
        out_ref[256 * b : 256 * b + 256, 0:COLS] = (scale * rows).astype(BF16)
    here = rank == 8.0
    scale = jnp.sum(jnp.where(here, gate, 0.0), axis=1, keepdims=True)
    rows = (scale * mm(onehot(here), tokens)).astype(BF16).astype(F32)
    extra[...] = jnp.zeros_like(extra)
    for q in range(5):
        extra[pl.ds(q, EXP, stride=8), :] = rows[:, 128 * q : 128 * q + 128]
    out_ref[:, COLS:WIDE] = extra[...].astype(BF16)


def choose(moves_ref, in_ref, out_ref):
    out_ref[...] = in_ref[...]
    for m in range(MOVES):
        out_ref[moves_ref[m]] = in_ref[moves_ref[MOVES + m]]


def last_rows(payload_ref, extra):
    extra[...] = payload_ref[:, COLS:WIDE].astype(F32)
    return jnp.concatenate(
        [extra[pl.ds(q, EXP, stride=8), :] for q in range(5)], axis=1
    ).astype(BF16)


def finish(
    payload_ref, one, two, first_hbm, master_hbm, second_hbm, out_hbm,
    first, master, second, weight, rows, extra, out, sems,
):
    me = lax.axis_index("tensor")
    copies, places = [], []
    for n, behind in enumerate((0, 1, 3, 2)):
        at = pl.ds(n * HPART, HPART)
        place = pl.ds(pl.multiple_of(lax.rem(me + 4 - behind, 4) * HPART, HPART), HPART)
        places.append(place)
        copies.append(pltpu.make_async_copy(first_hbm.at[at], first.at[at], sems.at[2 * n]))
        copies.append(
            pltpu.make_async_copy(master_hbm.at[place], master.at[at], sems.at[2 * n + 1])
        )
    copies.append(pltpu.make_async_copy(second_hbm, second, sems.at[8]))
    for copy in copies:
        copy.start()

    rows[0:MAIN, :] = payload_ref[:, 0:COLS]
    rows[MAIN:ROWS, :] = last_rows(payload_ref, extra)
    for n in range(4):
        at = slice(n * HPART, n * HPART + HPART)
        copies[2 * n].wait()
        gradient = mm(first[at, :], rows[...])
        copies[2 * n + 1].wait()
        moment_new = ONE_OLD * one[places[n], :].astype(F32) + ONE_NEW * gradient
        moment_two = TWO_OLD * two[places[n], :].astype(F32) + TWO_NEW * gradient * gradient
        root = moment_two * lax.rsqrt(moment_two)
        updated = KEEP * master[at, :] - moment_new * pl.reciprocal(root + EPSILON)
        weight[at, :] = updated.astype(BF16)
    copies[-1].wait()

    extra[...] = jnp.zeros_like(extra)
    sent = []
    for n, (start, stop) in enumerate(((0, 256), (256, 512), (512, 640))):
        total = mm(second[...], weight[:, start:stop]).astype(BF16)
        out[:, start:stop] = total[0:MAIN]
        ends = total[MAIN:ROWS].astype(F32)
        for q in range(start // 128, stop // 128):
            at = 128 * q - start
            extra[pl.ds(q, EXP, stride=8), :] = ends[:, at : at + 128]
        if stop == COLS:
            out[:, COLS:WIDE] = extra[...].astype(BF16)
            stop = WIDE
        cols = pl.ds(start, stop - start)
        sent.append(
            pltpu.make_async_copy(
                out.at[:, cols], out_hbm.at[:, cols], sems.at[9 + n]
            )
        )
        sent[-1].start()
    for copy in sent:
        copy.wait()


def mixing(route_ref, gates_ref, plan_ref, main_ref, last_ref):
    rank, gate = routed(route_ref[...], gates_ref[...], plan_ref[...])
    rank = rank.T
    gate = gate.T
    code = rank.astype(BF16)
    parts = thirds(gate)
    for b in range(4):
        c = iota((EXP, 256), 1)
        spread = onehot(iota((EXP, 256), 0) == 32 * b + c // 8)
        here = mm(code, spread) == (c % 8).astype(F32)
        for n, part in enumerate(parts):
            main_ref[128 * n : 128 * n + 128, 256 * b : 256 * b + 256] = jnp.where(
                here, mm(part, spread), 0.0
            ).astype(BF16)
    for n, part in enumerate(parts):
        last_ref[128 * n : 128 * n + 128, :] = jnp.where(
            rank == 8.0, part.astype(F32), 0.0
        ).astype(BF16)


def combine(main_ref, last_ref, payload_ref, out_ref, extra):
    total = mm(main_ref[...], payload_ref[:, 0:COLS]) + mm(
        last_ref[...], last_rows(payload_ref, extra)
    )
    out_ref[...] = (total[0:128] + (total[128:256] + total[256:384])).astype(BF16)


def shape(*extents, dtype=BF16):
    return jax.ShapeDtypeStruct(extents, dtype)


def exchange(x):
    return lax.all_to_all(x, "expert", split_axis=0, concat_axis=0, tiled=True)


def before(x, shift):
    return lax.ppermute(x, "tensor", [(i, (i + shift) % 4) for i in range(4)])


def gather(x):
    half = x.shape[0] // 2
    near, far = before(x, 1), before(x, 3)
    return [x, near, far, before(near[:half], 1), before(far[half:], 3)]


def shards(
    cotangent,
    route_first,
    gates_first,
    hidden_first,
    route_second,
    gates_second,
    hidden_second,
    master,
    moment_one,
    moment_two,
    old_plan,
    new_plan,
):
    labels = jnp.arange(EXP, dtype=jnp.int32)
    plan = old_plan.reshape(1, EXP)
    moved = old_plan != new_plan
    order = jnp.sum(jnp.where((labels[None, :] < labels[:, None]) & moved[None, :], 1, 0), axis=1)
    chosen = (order[None, :] == labels[:MOVES, None]) & moved[None, :]
    to = jnp.sum(jnp.where(chosen, labels[None, :], 0), axis=1)
    source = jnp.sum(jnp.where(new_plan[None, :] == old_plan[:, None], labels[None, :], 0), axis=1)
    origin = jnp.sum(jnp.where(labels[None, :] == to[:, None], source[None, :], 0), axis=1)
    moves = jnp.concatenate([to, origin])
    extra = pltpu.VMEM((MAIN, 128), F32)
    hbm = pl.BlockSpec(memory_space=pltpu.HBM)
    smem = pl.BlockSpec(memory_space=pltpu.SMEM)
    vmem = pl.BlockSpec(memory_space=pltpu.VMEM)

    with jax.named_scope("second_hidden_out"):
        tiles = hidden_second[0].T.reshape(24, 8, 9, 128).transpose(0, 2, 1, 3)
        tiles = jnp.pad(tiles.reshape(PROWS, 128), ((0, EXP * 14 - PROWS), (0, 0)))
        spread = exchange(tiles.reshape(EXP, *LEG))

    with jax.named_scope("dispatch"):
        rows = pl.pallas_call(
            build_rows,
            out_shape=shape(MAIN, WIDE),
            scratch_shapes=[extra],
            compiler_params=params(),
        )(route_first.T, gates_first.T, plan, cotangent)
    with jax.named_scope("second_hidden_in"):
        kept = pl.pallas_call(
            choose,
            out_shape=shape(EXP, *LEG),
            in_specs=[smem, vmem],
            compiler_params=params(),
        )(moves, spread)
        part = hidden_first[0].T
        kept, rows = lax.optimization_barrier((kept, rows))
        mine = exchange(kept).reshape(EXP * 14, 128)[:PROWS]
        mine = mine.reshape(24, 9, 8, 128).transpose(0, 2, 1, 3).reshape(HPART, ROWS)
        second = gather(mine)
        second = pl.pallas_call(
            prepare_second, out_shape=shape(ROWS, HID), compiler_params=params()
        )(*second)

    with jax.named_scope("dispatch"):
        arrived = exchange(rows.reshape(EXP, 8, WIDE)).reshape(MAIN, WIDE)

    with jax.named_scope("first_hidden"):
        first = pl.pallas_call(
            prepare_first, out_shape=shape(HID, ROWS), compiler_params=params()
        )(*gather(part))

    with jax.named_scope("mixing"):
        mix, mix_last = pl.pallas_call(
            mixing,
            out_shape=(shape(3 * TOK, MAIN), shape(3 * TOK, EXP)),
            compiler_params=params(),
        )(route_second.T, gates_second.T, plan)

    with jax.named_scope("finish"):
        produced = pl.pallas_call(
            finish,
            in_specs=[vmem, vmem, vmem, hbm, hbm, hbm],
            out_specs=hbm,
            out_shape=shape(MAIN, WIDE),
            scratch_shapes=[
                pltpu.VMEM((HID, ROWS), BF16),
                pltpu.VMEM((HID, COLS), F32),
                pltpu.VMEM((ROWS, HID), BF16),
                pltpu.VMEM((HID, COLS), BF16),
                pltpu.VMEM((ROWS, COLS), BF16),
                extra,
                pltpu.VMEM((MAIN, WIDE), BF16),
                pltpu.SemaphoreType.DMA((12,)),
            ],
            compiler_params=params(48),
        )(arrived, moment_one[0], moment_two[0], first, master[0], second)
        returned = exchange(produced.reshape(EXP, 8, WIDE)).reshape(MAIN, WIDE)

    with jax.named_scope("combine"):
        return pl.pallas_call(
            combine,
            out_shape=shape(TOK, COLS),
            scratch_shapes=[extra],
            compiler_params=params(),
        )(mix, mix_last, returned)


def solution(mesh):
    placed = (
        P("expert", "tensor"),
        P("expert", None),
        P("expert", None),
        P("expert", None, "tensor"),
        P("expert", None),
        P("expert", None),
        P("expert", None, "tensor"),
        P("expert", None, "tensor"),
        P("expert", None, "tensor"),
        P("expert", None, "tensor"),
        P(),
        P(),
    )
    return jax.shard_map(
        shards, mesh=mesh, in_specs=placed, out_specs=P("expert", "tensor"), check_vma=False
    )
```

```python
import jax
import jax.numpy as jnp
from jax import lax
from jax.experimental import pallas as pl
from jax.experimental.pallas import tpu as pltpu
from jax.sharding import PartitionSpec as P

BETA_ONE = 0.9
BETA_TWO = 0.95
CORRECT_ONE = 1.0 - 0.9**10
CORRECT_TWO = 1.0 - 0.95**10
LEARN_RATE = 0.04
WEIGHT_DECAY = 0.1
EPSILON = 1e-08
KEEP = 1.0 - LEARN_RATE * WEIGHT_DECAY
ONE_OLD = LEARN_RATE * BETA_ONE / CORRECT_ONE
ONE_NEW = LEARN_RATE * (1.0 - BETA_ONE) / CORRECT_ONE
TWO_OLD = BETA_TWO / CORRECT_TWO
TWO_NEW = (1.0 - BETA_TWO) / CORRECT_TWO

EXP = 128
TOK = 128
TOP = 6
CAP = 9
ROWS = EXP * CAP
MAIN = EXP * 8
HID = 768
HPART = 192
COLS = 640
WIDE = 768
PROWS = ROWS * HPART // 128
NONE = 99.0
LEG = (7, 2, 128)
MOVES = 8
F32 = jnp.float32
BF16 = jnp.bfloat16

NN = (((1,), (0,)), ((), ()))
NT = (((1,), (1,)), ((), ()))


def params(limit=16):
    return pltpu.CompilerParams(vmem_limit_bytes=limit * 1024 * 1024)


def iota(shape, dim):
    return lax.broadcasted_iota(jnp.int32, shape, dim)


def mm(a, b, dims=NN):
    return lax.dot_general(a, b, dims, preferred_element_type=F32)


def thirds(x):
    high = x.astype(BF16)
    rest = x - high.astype(F32)
    mid = rest.astype(BF16)
    low = (rest - mid.astype(F32)).astype(BF16)
    return high, mid, low


def routed(route, gates, plan):
    diag = iota((EXP, EXP), 0) == iota((EXP, EXP), 1)
    column = jnp.sum(jnp.where(diag, plan.astype(F32), 0.0), axis=1, keepdims=True)
    named = route.astype(F32)
    member = jnp.zeros((EXP, TOK), F32)
    gate = jnp.zeros((EXP, TOK), F32)
    for k in range(TOP):
        same = named[k : k + 1, :] == column
        member = jnp.where(same, 1.0, member)
        gate = jnp.where(same, gates[k : k + 1, :], gate)
    earlier = (iota((TOK, TOK), 0) < iota((TOK, TOK), 1)).astype(F32).astype(BF16)
    rank = mm(member.astype(BF16), earlier)
    return jnp.where(member > 0.0, rank, NONE), gate


def onehot(mask):
    return jnp.where(mask, 1.0, 0.0).astype(BF16)


def main_pick(block):
    r = iota((128, 256), 0)
    return onehot(iota((128, 256), 1) == 16 * block + (r // 8) * 9 + r % 8)


def last_pick():
    return onehot(iota((EXP, ROWS), 1) == iota((EXP, ROWS), 0) * 9 + 8)


def prepare_second(one_ref, three_ref, two_low_ref, two_high_ref, zero_ref, out_ref):
    refs = (one_ref, three_ref, two_low_ref, two_high_ref, zero_ref)
    whole = jnp.concatenate([ref[...] for ref in refs], axis=0)
    for b in range(8):
        win = slice(128 * b, 128 * b + 256)
        out_ref[128 * b : 128 * b + 128, :] = mm(main_pick(b), whole[:, win], NT).astype(BF16)
    out_ref[MAIN:ROWS, :] = mm(last_pick(), whole, NT).astype(BF16)


def prepare_first(h_ref, out_ref):
    for b in range(8):
        win = slice(128 * b, 128 * b + 256)
        out_ref[:, 128 * b : 128 * b + 128] = mm(h_ref[:, win], main_pick(b), NT).astype(BF16)
    out_ref[:, MAIN:ROWS] = mm(h_ref[...], last_pick(), NT).astype(BF16)


def build_rows(route_ref, gates_ref, plan_ref, tokens_ref, out_ref, extra):
    rank, gate = routed(route_ref[...], gates_ref[...], plan_ref[...])
    tokens = tokens_ref[...]
    high, mid, low = thirds(gate)
    code = rank.astype(BF16)
    for b in range(4):
        r = iota((256, EXP), 0)
        spread = onehot(iota((256, EXP), 1) == 32 * b + r // 8)
        here = mm(spread, code) == (r % 8).astype(F32)
        gates_here = (mm(spread, high) + mm(spread, mid)) + mm(spread, low)
        scale = jnp.sum(jnp.where(here, gates_here, 0.0), axis=1, keepdims=True)
        rows = mm(onehot(here), tokens)
        out_ref[256 * b : 256 * b + 256, 0:COLS] = (scale * rows).astype(BF16)
    here = rank == 8.0
    scale = jnp.sum(jnp.where(here, gate, 0.0), axis=1, keepdims=True)
    rows = (scale * mm(onehot(here), tokens)).astype(BF16).astype(F32)
    extra[...] = jnp.zeros_like(extra)
    for q in range(5):
        extra[pl.ds(q, EXP, stride=8), :] = rows[:, 128 * q : 128 * q + 128]
    out_ref[:, COLS:WIDE] = extra[...].astype(BF16)


def choose(moves_ref, in_ref, out_ref):
    out_ref[...] = in_ref[...]
    for m in range(MOVES):
        out_ref[moves_ref[m]] = in_ref[moves_ref[MOVES + m]]


def last_rows(payload_ref, extra):
    extra[...] = payload_ref[:, COLS:WIDE].astype(F32)
    return jnp.concatenate(
        [extra[pl.ds(q, EXP, stride=8), :] for q in range(5)], axis=1
    ).astype(BF16)


def finish(
    payload_ref, near_ref, far_ref, low_ref, high_ref, own_hbm, moments_hbm, master_hbm, second_hbm, out_hbm,
    own, moments, master, second, weight, gradients, rows, extra, out, sems,
):
    me = lax.axis_index("tensor")
    mine = pltpu.make_async_copy(own_hbm, own, sems.at[8])
    mine.start()
    copies = []
    for n, behind in enumerate((1, 3, 2, 0)):
        place = pl.ds(pl.multiple_of(lax.rem(me + 4 - behind, 4) * HPART, HPART), HPART)
        at = pl.ds(n * HPART, HPART)
        pair = (
            pltpu.make_async_copy(moments_hbm.at[:, place], moments.at[:, at], sems.at[2 * n]),
            pltpu.make_async_copy(master_hbm.at[place], master.at[at], sems.at[2 * n + 1]),
        )
        copies.append(pair)
        for copy in pair:
            copy.start()
    rest = pltpu.make_async_copy(second_hbm, second, sems.at[9])
    rest.start()

    rows[0:MAIN, :] = payload_ref[:, 0:COLS]
    rows[MAIN:ROWS, :] = last_rows(payload_ref, extra)
    at = 0
    for ref in (near_ref, far_ref, low_ref, high_ref, own):
        if ref is own:
            mine.wait()
        to = at + ref.shape[0]
        gradients[at:to, :] = mm(ref[...], rows[...])
        at = to
    for n in range(4):
        at = slice(n * HPART, n * HPART + HPART)
        for copy in copies[n]:
            copy.wait()
        gradient = gradients[at, :]
        moment_new = ONE_OLD * moments[0, at].astype(F32) + ONE_NEW * gradient
        moment_two = TWO_OLD * moments[1, at].astype(F32) + TWO_NEW * gradient * gradient
        root = moment_two * lax.rsqrt(moment_two)
        updated = KEEP * master[at, :] - moment_new * pl.reciprocal(root + EPSILON)
        weight[at, :] = updated.astype(BF16)
    rest.wait()

    extra[...] = jnp.zeros_like(extra)
    sent = []
    for n, (start, stop) in enumerate(((0, 256), (256, 512), (512, 640))):
        total = mm(second[...], weight[:, start:stop]).astype(BF16)
        out[:, start:stop] = total[0:MAIN]
        ends = total[MAIN:ROWS].astype(F32)
        for q in range(start // 128, stop // 128):
            at = 128 * q - start
            extra[pl.ds(q, EXP, stride=8), :] = ends[:, at : at + 128]
        if stop == COLS:
            out[:, COLS:WIDE] = extra[...].astype(BF16)
            stop = WIDE
        cols = pl.ds(start, stop - start)
        sent.append(
            pltpu.make_async_copy(
                out.at[:, cols], out_hbm.at[:, cols], sems.at[10 + n]
            )
        )
        sent[-1].start()
    for copy in sent:
        copy.wait()


def mixing(route_ref, gates_ref, plan_ref, main_ref, last_ref):
    rank, gate = routed(route_ref[...], gates_ref[...], plan_ref[...])
    rank = rank.T
    gate = gate.T
    code = rank.astype(BF16)
    parts = thirds(gate)
    for b in range(4):
        c = iota((EXP, 256), 1)
        spread = onehot(iota((EXP, 256), 0) == 32 * b + c // 8)
        here = mm(code, spread) == (c % 8).astype(F32)
        for n, part in enumerate(parts):
            main_ref[128 * n : 128 * n + 128, 256 * b : 256 * b + 256] = jnp.where(
                here, mm(part, spread), 0.0
            ).astype(BF16)
    for n, part in enumerate(parts):
        last_ref[128 * n : 128 * n + 128, :] = jnp.where(
            rank == 8.0, part.astype(F32), 0.0
        ).astype(BF16)


def combine(main_ref, last_ref, payload_ref, out_ref, extra):
    total = mm(main_ref[...], payload_ref[:, 0:COLS]) + mm(
        last_ref[...], last_rows(payload_ref, extra)
    )
    out_ref[...] = (total[0:128] + (total[128:256] + total[256:384])).astype(BF16)


def shape(*extents, dtype=BF16):
    return jax.ShapeDtypeStruct(extents, dtype)


def exchange(x):
    return lax.all_to_all(x, "expert", split_axis=0, concat_axis=0, tiled=True)


def before(x, shift):
    return lax.ppermute(x, "tensor", [(i, (i + shift) % 4) for i in range(4)])


def gather(x):
    half = x.shape[0] // 2
    near, far = before(x, 1), before(x, 3)
    return [near, far, before(near[:half], 1), before(far[half:], 3)]


def shards(
    cotangent,
    route_first,
    gates_first,
    hidden_first,
    route_second,
    gates_second,
    hidden_second,
    master,
    moment_one,
    moment_two,
    old_plan,
    new_plan,
):
    labels = jnp.arange(EXP, dtype=jnp.int32)
    plan = old_plan.reshape(1, EXP)
    moved = old_plan != new_plan
    order = jnp.sum(jnp.where((labels[None, :] < labels[:, None]) & moved[None, :], 1, 0), axis=1)
    chosen = (order[None, :] == labels[:MOVES, None]) & moved[None, :]
    to = jnp.sum(jnp.where(chosen, labels[None, :], 0), axis=1)
    source = jnp.sum(jnp.where(new_plan[None, :] == old_plan[:, None], labels[None, :], 0), axis=1)
    origin = jnp.sum(jnp.where(labels[None, :] == to[:, None], source[None, :], 0), axis=1)
    moves = jnp.concatenate([to, origin])
    extra = pltpu.VMEM((MAIN, 128), F32)
    hbm = pl.BlockSpec(memory_space=pltpu.HBM)
    smem = pl.BlockSpec(memory_space=pltpu.SMEM)
    vmem = pl.BlockSpec(memory_space=pltpu.VMEM)

    with jax.named_scope("second_hidden_out"):
        tiles = hidden_second[0].T.reshape(24, 8, 9, 128).transpose(0, 2, 1, 3)
        tiles = jnp.pad(tiles.reshape(PROWS, 128), ((0, EXP * 14 - PROWS), (0, 0)))
        spread = exchange(tiles.reshape(EXP, *LEG))

    with jax.named_scope("dispatch"):
        rows = pl.pallas_call(
            build_rows,
            out_shape=shape(MAIN, WIDE),
            scratch_shapes=[extra],
            compiler_params=params(),
        )(route_first.T, gates_first.T, plan, cotangent)
    with jax.named_scope("second_hidden_in"):
        kept = pl.pallas_call(
            choose,
            out_shape=shape(EXP, *LEG),
            in_specs=[smem, vmem],
            compiler_params=params(),
        )(moves, spread)
        part = pl.pallas_call(
            prepare_first, out_shape=shape(HPART, ROWS), compiler_params=params()
        )(hidden_first[0].T)
        moments = jnp.stack([moment_one[0], moment_two[0]])
        kept, rows, part, moments = lax.optimization_barrier((kept, rows, part, moments))
        mine = exchange(kept).reshape(EXP * 14, 128)[:PROWS]
        mine = mine.reshape(24, 9, 8, 128).transpose(0, 2, 1, 3).reshape(HPART, ROWS)
        second = [*gather(mine), mine]
        second = pl.pallas_call(
            prepare_second, out_shape=shape(ROWS, HID), compiler_params=params(), cost_estimate=pl.CostEstimate(flops=3*1000*1000000, bytes_accessed=0, transcendentals=0)
        )(*second)

    with jax.named_scope("dispatch"):
        arrived = exchange(rows.reshape(EXP, 8, WIDE)).reshape(MAIN, WIDE)

    with jax.named_scope("first_hidden"):
        first = gather(part)

    with jax.named_scope("mixing"):
        mix, mix_last = pl.pallas_call(
            mixing,
            out_shape=(shape(3 * TOK, MAIN), shape(3 * TOK, EXP)),
            compiler_params=params(),
        )(route_second.T, gates_second.T, plan)

    with jax.named_scope("finish"):
        produced = pl.pallas_call(
            finish,
            in_specs=[vmem] * 5 + [hbm] * 4,
            out_specs=hbm,
            out_shape=shape(MAIN, WIDE),
            scratch_shapes=[
                pltpu.VMEM((HPART, ROWS), BF16),
                pltpu.VMEM((2, HID, COLS), BF16),
                pltpu.VMEM((HID, COLS), F32),
                pltpu.VMEM((ROWS, HID), BF16),
                pltpu.VMEM((HID, COLS), BF16),
                pltpu.VMEM((HID, COLS), F32),
                pltpu.VMEM((ROWS, COLS), BF16),
                extra,
                pltpu.VMEM((MAIN, WIDE), BF16),
                pltpu.SemaphoreType.DMA((13,)),
            ],
            compiler_params=params(48),
        )(arrived, *first, part, moments, master[0], second)
        returned = exchange(produced.reshape(EXP, 8, WIDE)).reshape(MAIN, WIDE)

    with jax.named_scope("combine"):
        return pl.pallas_call(
            combine,
            out_shape=shape(TOK, COLS),
            scratch_shapes=[extra],
            compiler_params=params(),
        )(mix, mix_last, returned)


def solution(mesh):
    placed = (
        P("expert", "tensor"),
        P("expert", None),
        P("expert", None),
        P("expert", None, "tensor"),
        P("expert", None),
        P("expert", None),
        P("expert", None, "tensor"),
        P("expert", None, "tensor"),
        P("expert", None, "tensor"),
        P("expert", None, "tensor"),
        P(),
        P(),
    )
    return jax.shard_map(
        shards, mesh=mesh, in_specs=placed, out_specs=P("expert", "tensor"), check_vma=False
    )
```

```python
import jax
import jax.numpy as jnp
from jax import lax
from jax.experimental import pallas as pl
from jax.experimental.pallas import tpu as pltpu
from jax.sharding import PartitionSpec as P

BETA_ONE = 0.9
BETA_TWO = 0.95
CORRECT_ONE = 1.0 - 0.9**10
CORRECT_TWO = 1.0 - 0.95**10
LEARN_RATE = 0.04
WEIGHT_DECAY = 0.1
EPSILON = 1e-08
KEEP = 1.0 - LEARN_RATE * WEIGHT_DECAY
ONE_OLD = LEARN_RATE * BETA_ONE / CORRECT_ONE
ONE_NEW = LEARN_RATE * (1.0 - BETA_ONE) / CORRECT_ONE
TWO_OLD = BETA_TWO / CORRECT_TWO
TWO_NEW = (1.0 - BETA_TWO) / CORRECT_TWO

EXP = 128
TOK = 128
TOP = 6
CAP = 9
ROWS = EXP * CAP
MAIN = EXP * 8
HID = 768
HPART = 192
COLS = 640
WIDE = 768
PROWS = ROWS * HPART // 128
NONE = 99.0
LEG = (7, 2, 128)
MOVES = 8
F32 = jnp.float32
BF16 = jnp.bfloat16

NN = (((1,), (0,)), ((), ()))
NT = (((1,), (1,)), ((), ()))


def params(limit=16):
    return pltpu.CompilerParams(vmem_limit_bytes=limit * 1024 * 1024)


def iota(shape, dim):
    return lax.broadcasted_iota(jnp.int32, shape, dim)


def mm(a, b, dims=NN):
    return lax.dot_general(a, b, dims, preferred_element_type=F32)


def thirds(x):
    high = x.astype(BF16)
    rest = x - high.astype(F32)
    mid = rest.astype(BF16)
    low = (rest - mid.astype(F32)).astype(BF16)
    return high, mid, low


def routed(route, gates, plan):
    diag = iota((EXP, EXP), 0) == iota((EXP, EXP), 1)
    column = jnp.sum(jnp.where(diag, plan.astype(F32), 0.0), axis=1, keepdims=True)
    named = route.astype(F32)
    member = jnp.zeros((EXP, TOK), F32)
    gate = jnp.zeros((EXP, TOK), F32)
    for k in range(TOP):
        same = named[k : k + 1, :] == column
        member = jnp.where(same, 1.0, member)
        gate = jnp.where(same, gates[k : k + 1, :], gate)
    earlier = (iota((TOK, TOK), 0) < iota((TOK, TOK), 1)).astype(F32).astype(BF16)
    rank = mm(member.astype(BF16), earlier)
    return jnp.where(member > 0.0, rank, NONE), gate


def onehot(mask):
    return jnp.where(mask, 1.0, 0.0).astype(BF16)


def main_pick(block):
    r = iota((128, 256), 0)
    return onehot(iota((128, 256), 1) == 16 * block + (r // 8) * 9 + r % 8)


def last_pick():
    return onehot(iota((EXP, ROWS), 1) == iota((EXP, ROWS), 0) * 9 + 8)


def prepare_second(one_ref, three_ref, two_low_ref, two_high_ref, zero_ref, out_ref):
    refs = (one_ref, three_ref, two_low_ref, two_high_ref, zero_ref)
    whole = jnp.concatenate([ref[...] for ref in refs], axis=0)
    for b in range(8):
        win = slice(128 * b, 128 * b + 256)
        out_ref[128 * b : 128 * b + 128, :] = mm(main_pick(b), whole[:, win], NT).astype(BF16)
    out_ref[MAIN:ROWS, :] = mm(last_pick(), whole, NT).astype(BF16)


def prepare_first(h_ref, out_ref):
    for b in range(8):
        win = slice(128 * b, 128 * b + 256)
        out_ref[:, 128 * b : 128 * b + 128] = mm(h_ref[:, win], main_pick(b), NT).astype(BF16)
    out_ref[:, MAIN:ROWS] = mm(h_ref[...], last_pick(), NT).astype(BF16)


def build_rows(route_ref, gates_ref, plan_ref, tokens_ref, out_ref, extra):
    rank, gate = routed(route_ref[...], gates_ref[...], plan_ref[...])
    tokens = tokens_ref[...]
    high, mid, low = thirds(gate)
    code = rank.astype(BF16)
    for b in range(4):
        r = iota((256, EXP), 0)
        spread = onehot(iota((256, EXP), 1) == 32 * b + r // 8)
        here = mm(spread, code) == (r % 8).astype(F32)
        gates_here = (mm(spread, high) + mm(spread, mid)) + mm(spread, low)
        scale = jnp.sum(jnp.where(here, gates_here, 0.0), axis=1, keepdims=True)
        rows = mm(onehot(here), tokens)
        out_ref[256 * b : 256 * b + 256, 0:COLS] = (scale * rows).astype(BF16)
    here = rank == 8.0
    scale = jnp.sum(jnp.where(here, gate, 0.0), axis=1, keepdims=True)
    rows = (scale * mm(onehot(here), tokens)).astype(BF16).astype(F32)
    extra[...] = jnp.zeros_like(extra)
    for q in range(5):
        extra[pl.ds(q, EXP, stride=8), :] = rows[:, 128 * q : 128 * q + 128]
    out_ref[:, COLS:WIDE] = extra[...].astype(BF16)


def choose(moves_ref, in_ref, out_ref):
    out_ref[...] = in_ref[...]
    for m in range(MOVES):
        out_ref[moves_ref[m]] = in_ref[moves_ref[MOVES + m]]


def last_rows(payload_ref, extra):
    extra[...] = payload_ref[:, COLS:WIDE].astype(F32)
    return jnp.concatenate(
        [extra[pl.ds(q, EXP, stride=8), :] for q in range(5)], axis=1
    ).astype(BF16)


def finish(
    payload_ref, near_ref, far_ref, across_ref, own_hbm, moments_hbm, master_hbm, second_hbm, out_hbm,
    own, moments, master, second, weight, gradients, rows, extra, out, sems,
):
    me = lax.axis_index("tensor")
    mine = pltpu.make_async_copy(own_hbm, own, sems.at[8])
    mine.start()
    copies = []
    for n, behind in enumerate((1, 3, 2, 0)):
        place = pl.ds(pl.multiple_of(lax.rem(me + 4 - behind, 4) * HPART, HPART), HPART)
        at = pl.ds(n * HPART, HPART)
        pair = (
            pltpu.make_async_copy(moments_hbm.at[:, place], moments.at[:, at], sems.at[2 * n]),
            pltpu.make_async_copy(master_hbm.at[place], master.at[at], sems.at[2 * n + 1]),
        )
        copies.append(pair)
        for copy in pair:
            copy.start()
    rest = pltpu.make_async_copy(second_hbm, second, sems.at[9])
    rest.start()

    rows[0:MAIN, :] = payload_ref[:, 0:COLS]
    rows[MAIN:ROWS, :] = last_rows(payload_ref, extra)
    at = 0
    for ref in (near_ref, far_ref, across_ref, own):
        if ref is own:
            mine.wait()
        to = at + ref.shape[0]
        gradients[at:to, :] = mm(ref[...], rows[...])
        at = to
    for n in range(4):
        at = slice(n * HPART, n * HPART + HPART)
        for copy in copies[n]:
            copy.wait()
        gradient = gradients[at, :]
        moment_new = ONE_OLD * moments[0, at].astype(F32) + ONE_NEW * gradient
        moment_two = TWO_OLD * moments[1, at].astype(F32) + TWO_NEW * gradient * gradient
        root = moment_two * lax.rsqrt(moment_two)
        updated = KEEP * master[at, :] - moment_new * pl.reciprocal(root + EPSILON)
        weight[at, :] = updated.astype(BF16)
    rest.wait()

    extra[...] = jnp.zeros_like(extra)
    sent = []
    for n, (start, stop) in enumerate(((0, 256), (256, 512), (512, 640))):
        total = mm(second[...], weight[:, start:stop]).astype(BF16)
        out[:, start:stop] = total[0:MAIN]
        ends = total[MAIN:ROWS].astype(F32)
        for q in range(start // 128, stop // 128):
            at = 128 * q - start
            extra[pl.ds(q, EXP, stride=8), :] = ends[:, at : at + 128]
        if stop == COLS:
            out[:, COLS:WIDE] = extra[...].astype(BF16)
            stop = WIDE
        cols = pl.ds(start, stop - start)
        sent.append(
            pltpu.make_async_copy(
                out.at[:, cols], out_hbm.at[:, cols], sems.at[10 + n]
            )
        )
        sent[-1].start()
    for copy in sent:
        copy.wait()


def mixing(route_ref, gates_ref, plan_ref, main_ref, last_ref):
    rank, gate = routed(route_ref[...], gates_ref[...], plan_ref[...])
    rank = rank.T
    gate = gate.T
    code = rank.astype(BF16)
    parts = thirds(gate)
    for b in range(4):
        c = iota((EXP, 256), 1)
        spread = onehot(iota((EXP, 256), 0) == 32 * b + c // 8)
        here = mm(code, spread) == (c % 8).astype(F32)
        for n, part in enumerate(parts):
            main_ref[128 * n : 128 * n + 128, 256 * b : 256 * b + 256] = jnp.where(
                here, mm(part, spread), 0.0
            ).astype(BF16)
    for n, part in enumerate(parts):
        last_ref[128 * n : 128 * n + 128, :] = jnp.where(
            rank == 8.0, part.astype(F32), 0.0
        ).astype(BF16)


def combine(main_ref, last_ref, payload_ref, out_ref, extra):
    total = mm(main_ref[...], payload_ref[:, 0:COLS]) + mm(
        last_ref[...], last_rows(payload_ref, extra)
    )
    out_ref[...] = (total[0:128] + (total[128:256] + total[256:384])).astype(BF16)


def shape(*extents, dtype=BF16):
    return jax.ShapeDtypeStruct(extents, dtype)


def exchange(x):
    return lax.all_to_all(x, "expert", split_axis=0, concat_axis=0, tiled=True)


def before(x, shift):
    return lax.ppermute(x, "tensor", [(i, (i + shift) % 4) for i in range(4)])


def gather(x, halves):
    half = x.shape[0] // 2
    near, far = before(x, 1), before(x, 3)
    if halves:
        return [near, far, before(near[:half], 1), before(far[half:], 3)]
    return [near, far, before(near, 1)]


def shards(
    cotangent,
    route_first,
    gates_first,
    hidden_first,
    route_second,
    gates_second,
    hidden_second,
    master,
    moment_one,
    moment_two,
    old_plan,
    new_plan,
):
    labels = jnp.arange(EXP, dtype=jnp.int32)
    plan = old_plan.reshape(1, EXP)
    moved = old_plan != new_plan
    order = jnp.sum(jnp.where((labels[None, :] < labels[:, None]) & moved[None, :], 1, 0), axis=1)
    chosen = (order[None, :] == labels[:MOVES, None]) & moved[None, :]
    to = jnp.sum(jnp.where(chosen, labels[None, :], 0), axis=1)
    source = jnp.sum(jnp.where(new_plan[None, :] == old_plan[:, None], labels[None, :], 0), axis=1)
    origin = jnp.sum(jnp.where(labels[None, :] == to[:, None], source[None, :], 0), axis=1)
    moves = jnp.concatenate([to, origin])
    extra = pltpu.VMEM((MAIN, 128), F32)
    hbm = pl.BlockSpec(memory_space=pltpu.HBM)
    smem = pl.BlockSpec(memory_space=pltpu.SMEM)
    vmem = pl.BlockSpec(memory_space=pltpu.VMEM)

    with jax.named_scope("second_hidden_out"):
        tiles = hidden_second[0].T.reshape(24, 8, 9, 128).transpose(0, 2, 1, 3)
        tiles = jnp.pad(tiles.reshape(PROWS, 128), ((0, EXP * 14 - PROWS), (0, 0)))
        spread = exchange(tiles.reshape(EXP, *LEG))

    with jax.named_scope("dispatch"):
        rows = pl.pallas_call(
            build_rows,
            out_shape=shape(MAIN, WIDE),
            scratch_shapes=[extra],
            compiler_params=params(),
        )(route_first.T, gates_first.T, plan, cotangent)
    with jax.named_scope("second_hidden_in"):
        kept = pl.pallas_call(
            choose,
            out_shape=shape(EXP, *LEG),
            in_specs=[smem, vmem],
            compiler_params=params(),
        )(moves, spread)
        part = pl.pallas_call(
            prepare_first, out_shape=shape(HPART, ROWS), compiler_params=params()
        )(hidden_first[0].T)
        moments = jnp.stack([moment_one[0], moment_two[0]])
        kept, rows, part, moments = lax.optimization_barrier((kept, rows, part, moments))
        mine = exchange(kept).reshape(EXP * 14, 128)[:PROWS]
        mine = mine.reshape(24, 9, 8, 128).transpose(0, 2, 1, 3).reshape(HPART, ROWS)
        second = [*gather(mine, True), mine]
        second = pl.pallas_call(
            prepare_second, out_shape=shape(ROWS, HID), compiler_params=params(), cost_estimate=pl.CostEstimate(flops=3*1000*1000000, bytes_accessed=0, transcendentals=0)
        )(*second)

    with jax.named_scope("dispatch"):
        arrived = exchange(rows.reshape(EXP, 8, WIDE)).reshape(MAIN, WIDE)

    with jax.named_scope("first_hidden"):
        first = gather(part, False)

    with jax.named_scope("mixing"):
        mix, mix_last = pl.pallas_call(
            mixing,
            out_shape=(shape(3 * TOK, MAIN), shape(3 * TOK, EXP)),
            compiler_params=params(),
        )(route_second.T, gates_second.T, plan)

    with jax.named_scope("finish"):
        produced = pl.pallas_call(
            finish,
            in_specs=[vmem] * 4 + [hbm] * 4,
            out_specs=hbm,
            out_shape=shape(MAIN, WIDE),
            scratch_shapes=[
                pltpu.VMEM((HPART, ROWS), BF16),
                pltpu.VMEM((2, HID, COLS), BF16),
                pltpu.VMEM((HID, COLS), F32),
                pltpu.VMEM((ROWS, HID), BF16),
                pltpu.VMEM((HID, COLS), BF16),
                pltpu.VMEM((HID, COLS), F32),
                pltpu.VMEM((ROWS, COLS), BF16),
                extra,
                pltpu.VMEM((MAIN, WIDE), BF16),
                pltpu.SemaphoreType.DMA((13,)),
            ],
            compiler_params=params(48),
        )(arrived, *first, part, moments, master[0], second)
        returned = exchange(produced.reshape(EXP, 8, WIDE)).reshape(MAIN, WIDE)

    with jax.named_scope("combine"):
        return pl.pallas_call(
            combine,
            out_shape=shape(TOK, COLS),
            scratch_shapes=[extra],
            compiler_params=params(),
        )(mix, mix_last, returned)


def solution(mesh):
    placed = (
        P("expert", "tensor"),
        P("expert", None),
        P("expert", None),
        P("expert", None, "tensor"),
        P("expert", None),
        P("expert", None),
        P("expert", None, "tensor"),
        P("expert", None, "tensor"),
        P("expert", None, "tensor"),
        P("expert", None, "tensor"),
        P(),
        P(),
    )
    return jax.shard_map(
        shards, mesh=mesh, in_specs=placed, out_specs=P("expert", "tensor"), check_vma=False
    )
```

```python
import jax
import jax.numpy as jnp
from jax import lax
from jax.experimental import pallas as pl
from jax.experimental.pallas import tpu as pltpu
from jax.sharding import PartitionSpec as P

BETA_ONE = 0.9
BETA_TWO = 0.95
CORRECT_ONE = 1.0 - 0.9**10
CORRECT_TWO = 1.0 - 0.95**10
LEARN_RATE = 0.04
WEIGHT_DECAY = 0.1
EPSILON = 1e-08
KEEP = 1.0 - LEARN_RATE * WEIGHT_DECAY
ONE_OLD = LEARN_RATE * BETA_ONE / CORRECT_ONE
ONE_NEW = LEARN_RATE * (1.0 - BETA_ONE) / CORRECT_ONE
TWO_OLD = BETA_TWO / CORRECT_TWO
TWO_NEW = (1.0 - BETA_TWO) / CORRECT_TWO

EXP = 128
TOK = 128
TOP = 6
CAP = 9
ROWS = EXP * CAP
MAIN = EXP * 8
HID = 768
HPART = 192
COLS = 640
WIDE = 768
PROWS = ROWS * HPART // 128
NONE = 99.0
LEG = (7, 2, 128)
MOVES = 8
F32 = jnp.float32
BF16 = jnp.bfloat16

NN = (((1,), (0,)), ((), ()))
NT = (((1,), (1,)), ((), ()))


def params(limit=16):
    return pltpu.CompilerParams(vmem_limit_bytes=limit * 1024 * 1024)


def iota(shape, dim):
    return lax.broadcasted_iota(jnp.int32, shape, dim)


def mm(a, b, dims=NN):
    return lax.dot_general(a, b, dims, preferred_element_type=F32)


def thirds(x):
    high = x.astype(BF16)
    rest = x - high.astype(F32)
    mid = rest.astype(BF16)
    low = (rest - mid.astype(F32)).astype(BF16)
    return high, mid, low


def routed(route, gates, plan):
    diag = iota((EXP, EXP), 0) == iota((EXP, EXP), 1)
    column = jnp.sum(jnp.where(diag, plan.astype(F32), 0.0), axis=1, keepdims=True)
    named = route.astype(F32)
    member = jnp.zeros((EXP, TOK), F32)
    gate = jnp.zeros((EXP, TOK), F32)
    for k in range(TOP):
        same = named[k : k + 1, :] == column
        member = jnp.where(same, 1.0, member)
        gate = jnp.where(same, gates[k : k + 1, :], gate)
    earlier = (iota((TOK, TOK), 0) < iota((TOK, TOK), 1)).astype(F32).astype(BF16)
    rank = mm(member.astype(BF16), earlier)
    return jnp.where(member > 0.0, rank, NONE), gate


def onehot(mask):
    return jnp.where(mask, 1.0, 0.0).astype(BF16)


def main_pick(block):
    r = iota((128, 256), 0)
    return onehot(iota((128, 256), 1) == 16 * block + (r // 8) * 9 + r % 8)


def last_pick():
    return onehot(iota((EXP, ROWS), 1) == iota((EXP, ROWS), 0) * 9 + 8)


def prepare_second(one_ref, three_ref, two_low_ref, two_high_ref, zero_ref, out_ref):
    refs = (one_ref, three_ref, two_low_ref, two_high_ref, zero_ref)
    whole = jnp.concatenate([ref[...] for ref in refs], axis=0)
    for b in range(8):
        win = slice(128 * b, 128 * b + 256)
        out_ref[128 * b : 128 * b + 128, :] = mm(main_pick(b), whole[:, win], NT).astype(BF16)
    out_ref[MAIN:ROWS, :] = mm(last_pick(), whole, NT).astype(BF16)


def prepare_first(h_ref, out_ref):
    for b in range(8):
        win = slice(128 * b, 128 * b + 256)
        out_ref[:, 128 * b : 128 * b + 128] = mm(h_ref[:, win], main_pick(b), NT).astype(BF16)
    out_ref[:, MAIN:ROWS] = mm(h_ref[...], last_pick(), NT).astype(BF16)


def build_rows(route_ref, gates_ref, plan_ref, tokens_ref, out_ref, extra):
    rank, gate = routed(route_ref[...], gates_ref[...], plan_ref[...])
    tokens = tokens_ref[...]
    high, mid, low = thirds(gate)
    code = rank.astype(BF16)
    for b in range(4):
        r = iota((256, EXP), 0)
        spread = onehot(iota((256, EXP), 1) == 32 * b + r // 8)
        here = mm(spread, code) == (r % 8).astype(F32)
        gates_here = (mm(spread, high) + mm(spread, mid)) + mm(spread, low)
        scale = jnp.sum(jnp.where(here, gates_here, 0.0), axis=1, keepdims=True)
        rows = mm(onehot(here), tokens)
        out_ref[256 * b : 256 * b + 256, 0:COLS] = (scale * rows).astype(BF16)
    here = rank == 8.0
    scale = jnp.sum(jnp.where(here, gate, 0.0), axis=1, keepdims=True)
    rows = (scale * mm(onehot(here), tokens)).astype(BF16).astype(F32)
    extra[...] = jnp.zeros_like(extra)
    for q in range(5):
        extra[pl.ds(q, EXP, stride=8), :] = rows[:, 128 * q : 128 * q + 128]
    out_ref[:, COLS:WIDE] = extra[...].astype(BF16)


def choose(moves_ref, in_ref, out_ref):
    out_ref[...] = in_ref[...]
    for m in range(MOVES):
        out_ref[moves_ref[m]] = in_ref[moves_ref[MOVES + m]]


def last_rows(payload_ref, extra):
    extra[...] = payload_ref[:, COLS:WIDE].astype(F32)
    return jnp.concatenate(
        [extra[pl.ds(q, EXP, stride=8), :] for q in range(5)], axis=1
    ).astype(BF16)


def finish(
    payload_ref, near_ref, far_ref, low_ref, high_ref, own_hbm, moments_hbm, master_hbm, second_hbm, out_hbm,
    own, moments, master, second, weight, gradients, rows, extra, out, sems,
):
    me = lax.axis_index("tensor")
    mine = pltpu.make_async_copy(own_hbm, own, sems.at[8])
    mine.start()
    rest = pltpu.make_async_copy(second_hbm, second, sems.at[9])
    rest.start()
    copies = []
    for n, behind in enumerate((1, 3, 2, 0)):
        place = pl.ds(pl.multiple_of(lax.rem(me + 4 - behind, 4) * HPART, HPART), HPART)
        at = pl.ds(n * HPART, HPART)
        pair = (
            pltpu.make_async_copy(moments_hbm.at[:, place], moments.at[:, at], sems.at[2 * n]),
            pltpu.make_async_copy(master_hbm.at[place], master.at[at], sems.at[2 * n + 1]),
        )
        copies.append(pair)
        for copy in pair:
            copy.start()

    rows[0:MAIN, :] = payload_ref[:, 0:COLS]
    rows[MAIN:ROWS, :] = last_rows(payload_ref, extra)
    at = 0
    for ref in (near_ref, far_ref, low_ref, high_ref, own):
        if ref is own:
            mine.wait()
        to = at + ref.shape[0]
        gradients[at:to, :] = mm(ref[...], rows[...])
        at = to
    for n in range(4):
        at = slice(n * HPART, n * HPART + HPART)
        for copy in copies[n]:
            copy.wait()
        gradient = gradients[at, :]
        moment_new = ONE_OLD * moments[0, at].astype(F32) + ONE_NEW * gradient
        moment_two = TWO_OLD * moments[1, at].astype(F32) + TWO_NEW * gradient * gradient
        root = moment_two * lax.rsqrt(moment_two)
        updated = KEEP * master[at, :] - moment_new * pl.reciprocal(root + EPSILON)
        weight[at, :] = updated.astype(BF16)
    rest.wait()

    extra[...] = jnp.zeros_like(extra)
    sent = []
    for n, (start, stop) in enumerate(((0, 256), (256, 512), (512, 640))):
        total = mm(second[...], weight[:, start:stop]).astype(BF16)
        out[:, start:stop] = total[0:MAIN]
        ends = total[MAIN:ROWS].astype(F32)
        for q in range(start // 128, stop // 128):
            at = 128 * q - start
            extra[pl.ds(q, EXP, stride=8), :] = ends[:, at : at + 128]
        if stop == COLS:
            out[:, COLS:WIDE] = extra[...].astype(BF16)
            stop = WIDE
        cols = pl.ds(start, stop - start)
        sent.append(
            pltpu.make_async_copy(
                out.at[:, cols], out_hbm.at[:, cols], sems.at[10 + n]
            )
        )
        sent[-1].start()
    for copy in sent:
        copy.wait()


def mixing(route_ref, gates_ref, plan_ref, main_ref, last_ref):
    rank, gate = routed(route_ref[...], gates_ref[...], plan_ref[...])
    rank = rank.T
    gate = gate.T
    code = rank.astype(BF16)
    parts = thirds(gate)
    for b in range(4):
        c = iota((EXP, 256), 1)
        spread = onehot(iota((EXP, 256), 0) == 32 * b + c // 8)
        here = mm(code, spread) == (c % 8).astype(F32)
        for n, part in enumerate(parts):
            main_ref[128 * n : 128 * n + 128, 256 * b : 256 * b + 256] = jnp.where(
                here, mm(part, spread), 0.0
            ).astype(BF16)
    for n, part in enumerate(parts):
        last_ref[128 * n : 128 * n + 128, :] = jnp.where(
            rank == 8.0, part.astype(F32), 0.0
        ).astype(BF16)


def combine(main_ref, last_ref, payload_ref, out_ref, extra):
    total = mm(main_ref[...], payload_ref[:, 0:COLS]) + mm(
        last_ref[...], last_rows(payload_ref, extra)
    )
    out_ref[...] = (total[0:128] + (total[128:256] + total[256:384])).astype(BF16)


def shape(*extents, dtype=BF16):
    return jax.ShapeDtypeStruct(extents, dtype)


def exchange(x):
    return lax.all_to_all(x, "expert", split_axis=0, concat_axis=0, tiled=True)


def before(x, shift):
    return lax.ppermute(x, "tensor", [(i, (i + shift) % 4) for i in range(4)])


def gather(x):
    half = x.shape[0] // 2
    near, far = before(x, 1), before(x, 3)
    return [near, far, before(near[:half], 1), before(far[half:], 3)]


def shards(
    cotangent,
    route_first,
    gates_first,
    hidden_first,
    route_second,
    gates_second,
    hidden_second,
    master,
    moment_one,
    moment_two,
    old_plan,
    new_plan,
):
    labels = jnp.arange(EXP, dtype=jnp.int32)
    plan = old_plan.reshape(1, EXP)
    moved = old_plan != new_plan
    order = jnp.sum(jnp.where((labels[None, :] < labels[:, None]) & moved[None, :], 1, 0), axis=1)
    chosen = (order[None, :] == labels[:MOVES, None]) & moved[None, :]
    to = jnp.sum(jnp.where(chosen, labels[None, :], 0), axis=1)
    source = jnp.sum(jnp.where(new_plan[None, :] == old_plan[:, None], labels[None, :], 0), axis=1)
    origin = jnp.sum(jnp.where(labels[None, :] == to[:, None], source[None, :], 0), axis=1)
    moves = jnp.concatenate([to, origin])
    extra = pltpu.VMEM((MAIN, 128), F32)
    hbm = pl.BlockSpec(memory_space=pltpu.HBM)
    smem = pl.BlockSpec(memory_space=pltpu.SMEM)
    vmem = pl.BlockSpec(memory_space=pltpu.VMEM)

    with jax.named_scope("second_hidden_out"):
        tiles = hidden_second[0].T.reshape(24, 8, 9, 128).transpose(0, 2, 1, 3)
        tiles = jnp.pad(tiles.reshape(PROWS, 128), ((0, EXP * 14 - PROWS), (0, 0)))
        spread = exchange(tiles.reshape(EXP, *LEG))

    with jax.named_scope("dispatch"):
        rows = pl.pallas_call(
            build_rows,
            out_shape=shape(MAIN, WIDE),
            scratch_shapes=[extra],
            compiler_params=params(),
        )(route_first.T, gates_first.T, plan, cotangent)
    with jax.named_scope("second_hidden_in"):
        kept = pl.pallas_call(
            choose,
            out_shape=shape(EXP, *LEG),
            in_specs=[smem, vmem],
            compiler_params=params(),
        )(moves, spread)
        part = pl.pallas_call(
            prepare_first, out_shape=shape(HPART, ROWS), compiler_params=params()
        )(hidden_first[0].T)
        moments = jnp.stack([moment_one[0], moment_two[0]])
        kept, rows, part, moments = lax.optimization_barrier((kept, rows, part, moments))
        mine = exchange(kept).reshape(EXP * 14, 128)[:PROWS]
        mine = mine.reshape(24, 9, 8, 128).transpose(0, 2, 1, 3).reshape(HPART, ROWS)
        second = [*gather(mine), mine]
        second = pl.pallas_call(
            prepare_second, out_shape=shape(ROWS, HID), compiler_params=params(), cost_estimate=pl.CostEstimate(flops=3*1000*1000000, bytes_accessed=0, transcendentals=0)
        )(*second)

    with jax.named_scope("dispatch"):
        arrived = exchange(rows.reshape(EXP, 8, WIDE)).reshape(MAIN, WIDE)

    with jax.named_scope("first_hidden"):
        first = gather(part)

    with jax.named_scope("mixing"):
        mix, mix_last = pl.pallas_call(
            mixing,
            out_shape=(shape(3 * TOK, MAIN), shape(3 * TOK, EXP)),
            compiler_params=params(),
        )(route_second.T, gates_second.T, plan)

    with jax.named_scope("finish"):
        produced = pl.pallas_call(
            finish,
            in_specs=[vmem] * 5 + [hbm] * 4,
            out_specs=hbm,
            out_shape=shape(MAIN, WIDE),
            scratch_shapes=[
                pltpu.VMEM((HPART, ROWS), BF16),
                pltpu.VMEM((2, HID, COLS), BF16),
                pltpu.VMEM((HID, COLS), F32),
                pltpu.VMEM((ROWS, HID), BF16),
                pltpu.VMEM((HID, COLS), BF16),
                pltpu.VMEM((HID, COLS), F32),
                pltpu.VMEM((ROWS, COLS), BF16),
                extra,
                pltpu.VMEM((MAIN, WIDE), BF16),
                pltpu.SemaphoreType.DMA((13,)),
            ],
            compiler_params=params(48),
        )(arrived, *first, part, moments, master[0], second)
        returned = exchange(produced.reshape(EXP, 8, WIDE)).reshape(MAIN, WIDE)

    with jax.named_scope("combine"):
        return pl.pallas_call(
            combine,
            out_shape=shape(TOK, COLS),
            scratch_shapes=[extra],
            compiler_params=params(),
        )(mix, mix_last, returned)


def solution(mesh):
    placed = (
        P("expert", "tensor"),
        P("expert", None),
        P("expert", None),
        P("expert", None, "tensor"),
        P("expert", None),
        P("expert", None),
        P("expert", None, "tensor"),
        P("expert", None, "tensor"),
        P("expert", None, "tensor"),
        P("expert", None, "tensor"),
        P(),
        P(),
    )
    return jax.shard_map(
        shards, mesh=mesh, in_specs=placed, out_specs=P("expert", "tensor"), check_vma=False
    )
```
